32 devices in a mesh: section: 4 (over y, x), seq: 8 (over z, core), dp: 1.
Axes of the slice: x: 2, y: 2, z: 4, core: 2. Of those that a mesh axis runs over, the one named last changes fastest.
Arguments:
- roles: int32 [4], replicated, may hold values from 0 to 3, each once
- block_ids: int32 [2, 1, 1536], P(None, 'dp'), may hold values from 0 to 15, never falling along the last dimension, each value on 1 to 384 neighbouring positions
- latent: bfloat16 [1, 1536, 2560], P('dp', 'seq'), may hold values from -6 to 6
- pending: bfloat16 [1, 1536, 2560], P('dp', 'seq'), may hold values from -6 to 6
- context: float32 [1, 2560], P('dp'), may hold values from -6 to 6
- w_qkv: bfloat16 [3, 2560, 6144], P(None, None, 'seq'), may hold values from -3.3796842 to 3.3796842
- w_out: bfloat16 [3, 2048, 2560], P(None, 'seq'), may hold values from -0.125 to 0.125
- stored_attn: bfloat16 [1, 1536, 2048], P('dp', None, 'seq'), may hold values from -1.5 to 1.5
Outputs:
- block_out: bfloat16 [4, 1, 1536, 2560], P('section', 'dp', 'seq')
- dmd_grad: float32 [1, 1536, 2560], P('dp', 'seq')
- grad_out: float32 [2048, 2560], P('seq')
The draws below stay inside these ranges and needn't reach their ends.
Inputs may be any that keep to these rules, and one draw needn't show every extreme that they name: `roles`: each section has a different role: 0 generator, 1 teacher with context, 2 teacher without context, 3 fake-score model. `block_ids`: never falling along frames, starting at 0; each block has 1 to 384 frames, and one block of each row has exactly 384.
All inputs are finite; a program needn't handle non-finite values.
Results may differ from the reference program's by a relative error of at most 0.0083.
Values may be sent and summed in bfloat16 or wider, within the bound.
A program may use at most 128 MiB of HBM per device.

```python
import math
import jax
import jax.numpy as jnp
import numpy as np
from jax import lax

D = 2560
HEADS = 16
HEAD_DIM = 128
MODELS = 3
L = 1536
INNER = 2048
SPANS = 16
SPAN_MOST = 384
N_SECTION = 4
N_DP = 1


def draw_w_qkv(key, part):
    base = jax.random.normal(key, (MODELS, D, HEADS, 3, HEAD_DIM), jnp.float32)
    factors = jnp.array([2.0 ** 0.5, 2.0 ** 0.5, 1.0], jnp.float32)
    weights = jnp.clip(base, -5.0, 5.0) * D ** (-0.5) * factors[None, None, None, :, None]
    return weights.reshape(MODELS, D, 3 * HEADS * HEAD_DIM).astype(jnp.bfloat16)


def level_of(rng, shape, pieces, least, largest):
    def one(dim, shards_of):
        steps = jax.random.uniform(jax.random.fold_in(jax.random.fold_in(rng, 6), dim), (shards_of,), jnp.float32, least / len(pieces), largest / len(pieces))
        return jnp.repeat(jnp.exp(steps), shape[dim] // shards_of).reshape((-1,) + (1,) * (len(shape) - dim - 1))

    loudness = one(*pieces[0])
    for cut in pieces[1:]:
        loudness = loudness * one(*cut)
    return loudness


def split_up(number_of, total, most, slope):
    weights = [(1 << 20) // math.isqrt(standing ** slope) + 1 for standing in range(2, number_of + 1)]
    spare, counts = total - most - (number_of - 1), [1] * (number_of - 1)
    while spare > 0:
        free = [i for i in range(number_of - 1) if counts[i] < most]
        pool, left = sum([weights[i] for i in free]), spare
        for i in free:
            addition = min(most - counts[i], max(1, left * weights[i] // pool), spare)
            counts[i] = counts[i] + addition
            spare = spare - addition
    return np.array([most] + counts)


def uneven_parts(key, amount, total, most, lean):
    if amount == 2:
        one = jax.random.randint(key, (), max(1, total - most), min(most, total - 1) + 1)
        return jnp.stack([one, total - one])
    lengths = jnp.asarray(split_up(amount, total, most, lean), jnp.int32)
    couples = (amount - 1) // 2
    giver, taker = lengths[1:1 + 2 * couples:2], lengths[2:2 + 2 * couples:2]
    margin = jnp.minimum(giver - 1, most - taker)
    passed = jax.random.randint(jax.random.fold_in(key, 1), (couples,), 0, 1 << 20) % (margin + 1)
    lengths = lengths.at[1:1 + 2 * couples:2].set(giver - passed).at[2:2 + 2 * couples:2].set(taker + passed)
    return lengths[jax.random.permutation(jax.random.fold_in(key, 2), amount)]


def gaussian(rng, extent, width, bound, cuts=(), held_as=jnp.bfloat16):
    gain = level_of(rng, extent, cuts, -0.22, 0.18) if cuts else 1.0
    values = jax.random.normal(rng, extent, jnp.float32) * width * gain
    return jnp.minimum(jnp.maximum(values, -bound), bound).astype(held_as)


def setup_inputs(seed: int = 0) -> dict:
    key_list = jax.random.split(jax.random.key(seed), 9)
    roles = jax.random.permutation(key_list[0], 4).astype(jnp.int32)
    block_ids = jax.vmap(lambda own: jnp.searchsorted(jnp.cumsum(uneven_parts(own, SPANS, L, SPAN_MOST, 2)), jnp.arange(L), side="right"))(jax.random.split(key_list[1], 2 * N_DP)).reshape((2, N_DP, L)).astype(jnp.int32)
    latent = gaussian(key_list[2], (N_DP, L, D), 1.0, 6.0, ((1, 8),))
    pending = gaussian(key_list[3], (N_DP, L, D), 1.0, 6.0, ((1, 8),))
    context = gaussian(key_list[4], (N_DP, D), 1.0, 6.0, (), jnp.float32)
    w_qkv = draw_w_qkv(jax.random.fold_in(key_list[8], 71), 0)
    w_out = gaussian(key_list[6], (MODELS, INNER, D), INNER ** -0.5, 0.125, ((1, 8),))
    stored_attn = gaussian(key_list[7], (N_DP, L, INNER), 0.25, 1.5, ((2, 8),))
    return dict(roles=roles, block_ids=block_ids, latent=latent, pending=pending, context=context, w_qkv=w_qkv, w_out=w_out, stored_attn=stored_attn)


GUIDE = 3.0
EPSILON = 1e-06
NEGATIVE = -1e+30

def attend(qkv_rows, frame_ids):
    length = qkv_rows.shape[0]
    split = qkv_rows.reshape(length, HEADS, 3, HEAD_DIM).transpose(1, 2, 0, 3)
    block_size = min(512, length)
    block_count = length // block_size
    scale = HEAD_DIM ** (-0.5)

    def per_head(triple):
        queries = triple[0]
        keys_all = triple[1]
        values = triple[2]

        def per_block(args):
            query_rows, query_ids = args
            scores = lax.dot_general(query_rows, keys_all, (((1,), (1,)), ((), ())), preferred_element_type=jnp.float32) * scale
            visible = frame_ids[None, :] <= query_ids[:, None]
            scores = jnp.where(visible, scores, NEGATIVE)
            highest = lax.optimization_barrier(jnp.max(scores, axis=1, keepdims=True))
            expon = jnp.where(visible, jnp.exp(scores - highest), 0.0)
            probs = (expon / lax.optimization_barrier(jnp.sum(expon, axis=1, keepdims=True))).astype(jnp.bfloat16)
            return jnp.dot(probs, values, preferred_element_type=jnp.float32).astype(jnp.bfloat16)
        blocks = lax.map(per_block, (queries.reshape(block_count, block_size, HEAD_DIM), frame_ids.reshape(block_count, block_size)))
        return blocks.reshape(length, HEAD_DIM)
    heads_out = lax.map(per_head, split)
    return heads_out.transpose(1, 0, 2).reshape(length, HEADS * HEAD_DIM)

def reference(roles, block_ids, latent, pending, context, w_qkv, w_out, stored_attn):
    places = jnp.arange(4, dtype=jnp.int32)
    model_table = jnp.array([0, 1, 1, 2], jnp.int32)
    weight_table = jnp.array([0.0, -GUIDE, GUIDE - 1.0, 1.0], jnp.float32)
    section_outs = []
    gradient = jnp.zeros((N_DP, L, D), jnp.float32)
    for place in range(N_SECTION):
        section_role = roles[place]
        model_index = jnp.sum(jnp.where(places == section_role, model_table, 0)).astype(jnp.int32)
        score_weight = jnp.sum(jnp.where(places == section_role, weight_table, 0.0))
        w_in = lax.dynamic_index_in_dim(w_qkv, model_index, 0, keepdims=False)
        w_proj = lax.dynamic_index_in_dim(w_out, model_index, 0, keepdims=False)
        is_generator = section_role == 0
        with_context = jnp.logical_or(section_role == 1, section_role == 3).astype(jnp.float32)
        sequence_outs = []
        for seq_index in range(N_DP):
            scored = pending[seq_index].astype(jnp.float32) + with_context * context[seq_index][None, :]
            source = jnp.where(is_generator, latent[seq_index].astype(jnp.float32), scored)
            normed = (source * lax.rsqrt(lax.optimization_barrier(jnp.mean(source * source, axis=1, keepdims=True)) + EPSILON)).astype(jnp.bfloat16)
            qkv_rows = jnp.dot(normed, w_in, preferred_element_type=jnp.float32).astype(jnp.bfloat16)
            frame_ids = jnp.where(is_generator, block_ids[0, seq_index], block_ids[1, seq_index])
            attn = attend(qkv_rows, frame_ids)
            branch = jnp.dot(attn, w_proj, preferred_element_type=jnp.float32)
            sequence_outs.append((source + branch).astype(jnp.bfloat16))
            gradient = gradient.at[seq_index].add(score_weight * branch)
        section_outs.append(jnp.stack(sequence_outs))
    block_out = jnp.stack(section_outs)
    grad_bf = gradient.astype(jnp.bfloat16)
    grad_out = jnp.zeros((INNER, D), jnp.float32)
    for seq_index in range(N_DP):
        grad_out = grad_out + jnp.dot(stored_attn[seq_index].T, grad_bf[seq_index], preferred_element_type=jnp.float32)
    return (block_out, gradient, grad_out)
```

```python
import functools

import jax
import jax.numpy as jnp
from jax import lax
from jax.experimental import pallas as pl
from jax.experimental.pallas import tpu as pltpu
from jax.sharding import PartitionSpec as P

HEAD_DIM = 128
GUIDE = 3.0
EPSILON = 1e-06
NEGATIVE = -1e30
SPAN_MOST = 384
LOG2E = 1.4426950408889634


def attend_kernel(ids_col, ids_row, qkv, out):
    length = qkv.shape[0]
    heads = qkv.shape[1] // (3 * HEAD_DIM)
    rows = min(256, length)
    factor = HEAD_DIM ** (-0.5) * LOG2E
    for block in range(length // rows):
        first = block * rows
        seen = min(length, first + rows + SPAN_MOST)
        hidden = ids_row[:, :seen] > ids_col[first:first + rows, :]
        for head in range(heads):
            base = head * 3 * HEAD_DIM
            query = qkv[first:first + rows, base:base + HEAD_DIM]
            keys = qkv[:seen, base + HEAD_DIM:base + 2 * HEAD_DIM]
            values = qkv[:seen, base + 2 * HEAD_DIM:base + 3 * HEAD_DIM]
            scores = lax.dot_general(
                query, keys, (((1,), (1,)), ((), ())), preferred_element_type=jnp.float32
            )
            scores = jnp.where(hidden, NEGATIVE, scores)
            highest = jnp.max(scores, axis=1, keepdims=True)
            expon = jnp.exp2((scores - highest) * factor)
            total = jnp.sum(expon, axis=1, keepdims=True)
            mixed = jnp.dot(
                expon.astype(jnp.bfloat16), values, preferred_element_type=jnp.float32
            )
            out[first:first + rows, head * HEAD_DIM:(head + 1) * HEAD_DIM] = (
                mixed / total
            ).astype(jnp.bfloat16)


def attend(qkv_rows, frame_ids):
    length, width = qkv_rows.shape
    heads = width // (3 * HEAD_DIM)
    vmem = pl.BlockSpec(memory_space=pltpu.VMEM)
    return pl.pallas_call(
        attend_kernel,
        out_shape=jax.ShapeDtypeStruct((length, heads * HEAD_DIM), jnp.bfloat16),
        in_specs=[vmem] * 3,
        out_specs=vmem,
        compiler_params=pltpu.CompilerParams(vmem_limit_bytes=48 << 20),
        cost_estimate=pl.CostEstimate(
            flops=4 * length * length * HEAD_DIM * heads,
            bytes_accessed=qkv_rows.size * 3,
            transcendentals=length * length * heads,
        ),
    )(frame_ids[:, None], frame_ids[None, :], qkv_rows)


def per_device(roles, block_ids, latent, pending, context, w_qkv, w_out, stored_attn):
    section = lax.axis_index("section")
    sections = lax.axis_size("section")
    places = jnp.arange(4, dtype=jnp.int32)
    weight_table = jnp.array([0.0, -GUIDE, GUIDE - 1.0, 1.0], jnp.float32)
    section_role = jnp.sum(jnp.where(places == section, roles, 0))
    model_index = jnp.sum(jnp.where(places == section_role, jnp.array([0, 1, 1, 2], jnp.int32), 0))
    score_weight = jnp.sum(jnp.where(places == section_role, weight_table, 0.0))
    w_in = lax.dynamic_index_in_dim(w_qkv, model_index, 0, keepdims=False)
    w_proj = lax.dynamic_index_in_dim(w_out, model_index, 0, keepdims=False)
    is_generator = section_role == 0
    with_context = jnp.logical_or(section_role == 1, section_role == 3).astype(jnp.float32)
    width = latent.shape[2]
    scored = pending[0].astype(jnp.float32) + with_context * context[0][None, :]
    source = jnp.where(is_generator, latent[0].astype(jnp.float32), scored)
    normed = (
        source * lax.rsqrt(jnp.mean(source * source, axis=1, keepdims=True) + EPSILON)
    ).astype(jnp.bfloat16)
    qkv_rows = jnp.dot(
        lax.all_gather(normed, "seq", axis=0, tiled=True), w_in, preferred_element_type=jnp.float32
    ).astype(jnp.bfloat16)
    frame_ids = jnp.where(is_generator, block_ids[0, 0], block_ids[1, 0])
    attn = attend(qkv_rows, frame_ids)
    local_attn = lax.all_to_all(attn, "seq", split_axis=0, concat_axis=1, tiled=True)
    branch = jnp.dot(
        local_attn,
        lax.all_gather(w_proj, "seq", axis=0, tiled=True),
        preferred_element_type=jnp.float32,
    )
    block_out = (source + branch).astype(jnp.bfloat16)[None, None]
    rows = branch.shape[0]
    quarter = width // sections
    terms = (score_weight * branch).astype(jnp.bfloat16)
    terms = terms.reshape(rows, sections, quarter).transpose(1, 0, 2)
    terms = lax.all_to_all(terms, "section", split_axis=0, concat_axis=0, tiled=True)
    grad_bf = jnp.sum(terms.astype(jnp.float32), axis=0).astype(jnp.bfloat16)
    gradient = lax.all_gather(grad_bf, "section", axis=1, tiled=True).astype(jnp.float32)
    grad_rows = lax.all_gather(grad_bf, "seq", axis=0, tiled=True)
    local_grad = lax.dot_general(
        stored_attn[0], grad_rows, (((0,), (0,)), ((), ())), preferred_element_type=jnp.float32
    )
    local_grad = lax.psum(local_grad, "dp").astype(jnp.bfloat16)
    grad_out = lax.all_gather(local_grad, "section", axis=1, tiled=True).astype(jnp.float32)
    return (block_out, gradient[None], grad_out)


def solution(mesh):
    placed = (
        P(),
        P(None, "dp", None),
        P("dp", "seq", None),
        P("dp", "seq", None),
        P("dp", None),
        P(None, None, "seq"),
        P(None, "seq", None),
        P("dp", None, "seq"),
    )
    return jax.shard_map(
        per_device,
        mesh=mesh,
        in_specs=placed,
        out_specs=(P("section", "dp", "seq", None), P("dp", "seq", None), P("seq", None)),
        check_vma=False,
    )
```

```python
import functools

import jax
import jax.numpy as jnp
from jax import lax
from jax.experimental import pallas as pl
from jax.experimental.pallas import tpu as pltpu
from jax.sharding import PartitionSpec as P

HEAD_DIM = 128
GUIDE = 3.0
EPSILON = 1e-06
NEGATIVE = -1e30
SPAN_MOST = 384
LOG2E = 1.4426950408889634
MESH = pl.DeviceIdType.MESH


def attend_kernel(ids_col, ids_row, qkv, out):
    length = qkv.shape[0]
    heads = qkv.shape[1] // (3 * HEAD_DIM)
    rows = min(256, length)
    factor = HEAD_DIM ** (-0.5) * LOG2E
    for block in range(length // rows):
        first = block * rows
        seen = min(length, first + rows + SPAN_MOST)
        hidden = ids_row[:, :seen] > ids_col[first:first + rows, :]
        for head in range(heads):
            base = head * 3 * HEAD_DIM
            query = qkv[first:first + rows, base:base + HEAD_DIM]
            keys = qkv[:seen, base + HEAD_DIM:base + 2 * HEAD_DIM]
            values = qkv[:seen, base + 2 * HEAD_DIM:base + 3 * HEAD_DIM]
            scores = lax.dot_general(
                query, keys, (((1,), (1,)), ((), ())), preferred_element_type=jnp.float32
            )
            scores = jnp.where(hidden, NEGATIVE, scores)
            highest = jnp.max(scores, axis=1, keepdims=True)
            expon = jnp.exp2((scores - highest) * factor)
            total = jnp.sum(expon, axis=1, keepdims=True)
            mixed = jnp.dot(
                expon.astype(jnp.bfloat16), values, preferred_element_type=jnp.float32
            )
            out[first:first + rows, head * HEAD_DIM:(head + 1) * HEAD_DIM] = (
                mixed / total
            ).astype(jnp.bfloat16)


def attend(qkv_rows, frame_ids):
    length, width = qkv_rows.shape
    heads = width // (3 * HEAD_DIM)
    vmem = pl.BlockSpec(memory_space=pltpu.VMEM)
    return pl.pallas_call(
        attend_kernel,
        out_shape=jax.ShapeDtypeStruct((length, heads * HEAD_DIM), jnp.bfloat16),
        in_specs=[vmem] * 3,
        out_specs=vmem,
        compiler_params=pltpu.CompilerParams(vmem_limit_bytes=48 << 20),
        cost_estimate=pl.CostEstimate(
            flops=4 * length * length * HEAD_DIM * heads,
            bytes_accessed=qkv_rows.size * 3,
            transcendentals=length * length * heads,
        ),
    )(frame_ids[:, None], frame_ids[None, :], qkv_rows)


def device_at(section=None, seq=None):
    place = {}
    if section is not None:
        place["section"] = section
    if seq is not None:
        place["seq"] = seq
    return place


def greet(peers):
    barrier = pltpu.get_barrier_semaphore()
    count = 0
    for condition, device in peers:
        if condition is None:
            pl.semaphore_signal(barrier, inc=1, device_id=device, device_id_type=MESH)
            count = count + 1
        else:
            @pl.when(condition)
            def _(device=device):
                pl.semaphore_signal(barrier, inc=1, device_id=device, device_id_type=MESH)

            count = count + condition.astype(jnp.int32)
    pl.semaphore_wait(barrier, count)


def remote(src, dst, send, recv, device):
    return pltpu.make_async_remote_copy(
        src_ref=src, dst_ref=dst, send_sem=send, recv_sem=recv,
        device_id=device, device_id_type=MESH,
    )


def tail_kernel(
    sections, line, finish,
    scale, attn, w2, source, stored,
    block_out, dmd, grad_out,
    attn_sib, w_sib, arrived, leaving, res_out, branch, terms, parts, grads, lines, finals,
    core_send, core_recv, sum_send, sum_recv, plane_send, plane_recv,
    line_send, line_recv, sib_send, sib_recv,
):
    section = lax.axis_index("section")
    me = lax.axis_index("seq")
    z, core = lax.div(me, 2), lax.rem(me, 2)
    sibling = device_at(seq=2 * z + 1 - core)
    above = device_at(seq=jnp.minimum(me + 2, 2 * line - 1))
    below = device_at(seq=jnp.maximum(me - 2, 0))
    plane = [device_at(section=lax.rem(section + d, sections)) for d in range(1, sections)]
    has_above, has_below = z < line - 1, z > 0
    greet([(None, sibling), (has_above, above), (has_below, below)] + [(None, p) for p in plane])

    rows = source.shape[0]
    both = 2 * rows
    half = w2.shape[2]
    quarter = terms.shape[2]
    tile = 256 if half % 256 == 0 else 128

    w_copy = remote(w2.at[1 - core], w_sib, core_send.at[0], core_recv.at[0], sibling)
    a_copy = remote(attn, attn_sib, core_send.at[1], core_recv.at[1], sibling)
    w_copy.start()
    a_copy.start()
    w_copy.wait()
    a_copy.wait()

    def product(first, amount, column):
        span = pl.ds(pl.multiple_of(first, rows), amount)
        return jnp.dot(
            attn[span, :], w2[core, :, pl.ds(column, tile)], preferred_element_type=jnp.float32
        ) + jnp.dot(
            attn_sib[span, :], w_sib[:, pl.ds(column, tile)], preferred_element_type=jnp.float32
        )

    def sum_copy(way, target):
        return remote(
            leaving.at[target], arrived.at[way, target],
            sum_send.at[way, target], sum_recv.at[way, target],
            above if way == 0 else below,
        )

    def push(way, target, has_before):
        @pl.when(has_before)
        def _():
            sum_copy(way, target).wait_recv()

        for column in range(0, half, tile):
            value = product(target * both, both, column)
            before = arrived[way, target, :, pl.ds(column, tile)].astype(jnp.float32)
            value = value + jnp.where(has_before, before, 0.0)
            leaving[target, :, pl.ds(column, tile)] = value.astype(jnp.bfloat16)
        sum_copy(way, target).start()

    def step(tau, carry):
        @pl.when(tau >= z)
        def _():
            push(0, line - 1 - tau + z, has_below)

        @pl.when(tau >= line - 1 - z)
        def _():
            push(1, tau - (line - 1 - z), has_above)

        return carry

    lax.fori_loop(0, line - 1, step, 0)

    @pl.when(has_below)
    def _():
        sum_copy(0, z).wait_recv()

    @pl.when(has_above)
    def _():
        sum_copy(1, z).wait_recv()

    def own(which, store):
        span = pl.ds(pl.multiple_of(which * rows, rows), rows)
        for column in range(0, half, tile):
            value = product(z * both + which * rows, rows, column)
            up = arrived[0, z, span, pl.ds(column, tile)].astype(jnp.float32)
            down = arrived[1, z, span, pl.ds(column, tile)].astype(jnp.float32)
            store(column, value + jnp.where(has_below, up, 0.0) + jnp.where(has_above, down, 0.0))

    def to_sibling(column, value):
        res_out[:, pl.ds(column, tile)] = value

    def to_branch(column, value):
        branch[core, :, pl.ds(column, tile)] = value

    own(1 - core, to_sibling)
    res_copy = remote(res_out, branch.at[core], core_send.at[2], core_recv.at[2], sibling)
    res_copy.start()
    own(core, to_branch)
    res_copy.wait_send()
    remote(res_out, branch.at[1 - core], core_send.at[2], core_recv.at[2], sibling).wait_recv()

    per_half = half // quarter
    for q in range(sections):
        low = (q % per_half) * quarter
        terms[q] = (scale[0, 0] * branch[q // per_half, :, low:low + quarter]).astype(jnp.bfloat16)

    def plane_copies(phase, src, dst):
        return [
            remote(src(lax.rem(section + d, sections)), dst(d),
                   plane_send.at[phase, d - 1], plane_recv.at[phase, d - 1], plane[d - 1])
            for d in range(1, sections)
        ]

    sends = plane_copies(0, lambda to: terms.at[to], lambda d: parts.at[d - 1])
    for copy in sends:
        copy.start()
    for h in range(2):
        columns = slice(h * half, (h + 1) * half)
        block_out[:, columns] = (source[:, columns] + branch[h]).astype(jnp.bfloat16)
    total = terms[section].astype(jnp.float32)
    for d in range(1, sections):
        sends[d - 1].wait()
        total = total + parts[d - 1].astype(jnp.float32)
    grad = total.astype(jnp.bfloat16)
    lines[z, core] = grad
    grads[section] = grad

    def line_copy(way, block):
        return remote(
            lines.at[block, core], lines.at[block, core],
            line_send.at[way, block], line_recv.at[way, block], above if way == 0 else below,
        )

    def sib_copy(block):
        return remote(
            lines.at[block, core], lines.at[block, core],
            sib_send.at[block], sib_recv.at[block], sibling,
        )

    @pl.when(has_above)
    def _():
        line_copy(0, z).start()

    @pl.when(has_below)
    def _():
        line_copy(1, z).start()

    sib_copy(z).start()

    def gather(phase, buffer):
        copies = plane_copies(phase, lambda to: buffer.at[section], lambda d: buffer.at[section])
        for copy in copies:
            copy.start()
        return copies

    def gathered(phase, buffer, copies):
        for d in range(1, sections):
            copies[d - 1].wait_send()
            slot = buffer.at[lax.rem(section + sections - d, sections)]
            remote(slot, slot, plane_send.at[phase, d - 1], plane_recv.at[phase, d - 1],
                   plane[d - 1]).wait_recv()

    copies = gather(1, grads)
    for k in range(1, line):
        @pl.when(z >= k)
        def _(k=k):
            line_copy(0, z - k).wait_recv()

            @pl.when(has_above)
            def _():
                line_copy(0, z - k).start()

            sib_copy(z - k).start()

        @pl.when(z + k < line)
        def _(k=k):
            line_copy(1, z + k).wait_recv()

            @pl.when(has_below)
            def _():
                line_copy(1, z + k).start()

            sib_copy(z + k).start()

    def sib_wait(block, carry):
        slot = lines.at[block, 1 - core]
        sib_copy(block).wait_send()
        remote(slot, slot, sib_send.at[block], sib_recv.at[block], sibling).wait_recv()
        return carry

    lax.fori_loop(0, line, sib_wait, 0)
    everything = lines[...].reshape(line * both, quarter)
    local = jnp.dot(stored[...], everything, preferred_element_type=jnp.float32)
    if finish:
        finals[section] = local.astype(jnp.bfloat16)
        last = gather(2, finals)
    else:
        grad_out[...] = local
    gathered(1, grads, copies)
    for q in range(sections):
        dmd[:, q * quarter:(q + 1) * quarter] = grads[q].astype(jnp.float32)

    def line_drain(block, carry):
        @pl.when(jnp.logical_and(block <= z, has_above))
        def _():
            line_copy(0, block).wait_send()

        @pl.when(jnp.logical_and(block >= z, has_below))
        def _():
            line_copy(1, block).wait_send()

        @pl.when(block > z)
        def _():
            sum_copy(0, block).wait_send()

        @pl.when(block < z)
        def _():
            sum_copy(1, block).wait_send()

        return carry

    lax.fori_loop(0, line, line_drain, 0)
    if finish:
        gathered(2, finals, last)
        for q in range(sections):
            grad_out[:, q * quarter:(q + 1) * quarter] = finals[q].astype(jnp.float32)


def tail(scale, attn, w_proj, source, stored, finish):
    sections, seq = lax.axis_size("section"), lax.axis_size("seq")
    line = seq // 2
    rows, width = source.shape
    length, inner = attn.shape
    half, quarter = width // 2, width // sections
    w2 = w_proj.reshape(inner, 2, half).transpose(1, 0, 2)
    vmem = pl.BlockSpec(memory_space=pltpu.VMEM)
    smem = pl.BlockSpec(memory_space=pltpu.SMEM)
    bf, f32 = jnp.bfloat16, jnp.float32
    dma = pltpu.SemaphoreType.DMA
    return pl.pallas_call(
        functools.partial(tail_kernel, sections, line, finish),
        out_shape=(
            jax.ShapeDtypeStruct((rows, width), bf),
            jax.ShapeDtypeStruct((rows, width), f32),
            jax.ShapeDtypeStruct((inner, width if finish else quarter), f32),
        ),
        in_specs=[smem] + [vmem] * 4,
        out_specs=(vmem,) * 3,
        scratch_shapes=[
            pltpu.VMEM((length, inner), bf),
            pltpu.VMEM((inner, half), bf),
            pltpu.VMEM((2, line, 2 * rows, half), bf),
            pltpu.VMEM((line, 2 * rows, half), bf),
            pltpu.VMEM((rows, half), f32),
            pltpu.VMEM((2, rows, half), f32),
            pltpu.VMEM((sections, rows, quarter), bf),
            pltpu.VMEM((sections - 1, rows, quarter), bf),
            pltpu.VMEM((sections, rows, quarter), bf),
            pltpu.VMEM((line, 2, rows, quarter), bf),
            pltpu.VMEM((sections, inner, quarter), bf),
            dma((3,)), dma((3,)),
            dma((2, line)), dma((2, line)),
            dma((3, sections - 1)), dma((3, sections - 1)),
            dma((2, line)), dma((2, line)),
            dma((line,)), dma((line,)),
        ],
        compiler_params=pltpu.CompilerParams(
            collective_id=1, has_side_effects=True, vmem_limit_bytes=56 << 20
        ),
        cost_estimate=pl.CostEstimate(
            flops=2 * length * inner * width, bytes_accessed=8 << 20, transcendentals=0
        ),
    )(scale, attn, w2, source, stored)


def per_device(roles, block_ids, latent, pending, context, w_qkv, w_out, stored_attn):
    section = lax.axis_index("section")
    places = jnp.arange(4, dtype=jnp.int32)
    weight_table = jnp.array([0.0, -GUIDE, GUIDE - 1.0, 1.0], jnp.float32)
    section_role = jnp.sum(jnp.where(places == section, roles, 0))
    model_index = jnp.sum(jnp.where(places == section_role, jnp.array([0, 1, 1, 2], jnp.int32), 0))
    score_weight = jnp.sum(jnp.where(places == section_role, weight_table, 0.0))
    w_in = lax.dynamic_index_in_dim(w_qkv, model_index, 0, keepdims=False)
    w_proj = lax.dynamic_index_in_dim(w_out, model_index, 0, keepdims=False)
    is_generator = section_role == 0
    with_context = jnp.logical_or(section_role == 1, section_role == 3).astype(jnp.float32)
    scored = pending[0].astype(jnp.float32) + with_context * context[0][None, :]
    source = jnp.where(is_generator, latent[0].astype(jnp.float32), scored)
    normed = (
        source * lax.rsqrt(jnp.mean(source * source, axis=1, keepdims=True) + EPSILON)
    ).astype(jnp.bfloat16)
    qkv_rows = jnp.dot(
        lax.all_gather(normed, "seq", axis=0, tiled=True), w_in, preferred_element_type=jnp.float32
    ).astype(jnp.bfloat16)
    frame_ids = jnp.where(is_generator, block_ids[0, 0], block_ids[1, 0])
    attn = attend(qkv_rows, frame_ids)
    finish = lax.axis_size("dp") == 1
    block_out, gradient, grad_out = tail(
        score_weight.reshape(1, 1), attn, w_proj, source, stored_attn[0].T, finish
    )
    if not finish:
        grad_out = lax.psum(grad_out, "dp").astype(jnp.bfloat16)
        grad_out = lax.all_gather(grad_out, "section", axis=1, tiled=True).astype(jnp.float32)
    return (block_out[None, None], gradient[None], grad_out)


def solution(mesh):
    placed = (
        P(),
        P(None, "dp", None),
        P("dp", "seq", None),
        P("dp", "seq", None),
        P("dp", None),
        P(None, None, "seq"),
        P(None, "seq", None),
        P("dp", None, "seq"),
    )
    return jax.shard_map(
        per_device,
        mesh=mesh,
        in_specs=placed,
        out_specs=(P("section", "dp", "seq", None), P("dp", "seq", None), P("seq", None)),
        check_vma=False,
    )
```

```python
import functools

import jax
import jax.numpy as jnp
from jax import lax
from jax.experimental import pallas as pl
from jax.experimental.pallas import tpu as pltpu
from jax.sharding import PartitionSpec as P

HEAD_DIM = 128
GUIDE = 3.0
EPSILON = 1e-06
NEGATIVE = -1e30
SPAN_MOST = 384
LOG2E = 1.4426950408889634
MESH = pl.DeviceIdType.MESH


def attend_kernel(ids_col, ids_row, qkv, out):
    length = qkv.shape[0]
    heads = qkv.shape[1] // (3 * HEAD_DIM)
    rows = min(256, length)
    factor = HEAD_DIM ** (-0.5) * LOG2E
    for block in range(length // rows):
        first = block * rows
        seen = min(length, first + rows + SPAN_MOST)
        hidden = ids_row[:, :seen] > ids_col[first:first + rows, :]
        for head in range(heads):
            base = head * 3 * HEAD_DIM
            query = qkv[first:first + rows, base:base + HEAD_DIM]
            keys = qkv[:seen, base + HEAD_DIM:base + 2 * HEAD_DIM]
            values = qkv[:seen, base + 2 * HEAD_DIM:base + 3 * HEAD_DIM]
            scores = lax.dot_general(
                query, keys, (((1,), (1,)), ((), ())), preferred_element_type=jnp.float32
            )
            scores = jnp.where(hidden, NEGATIVE, scores)
            highest = jnp.max(scores, axis=1, keepdims=True)
            expon = jnp.exp2((scores - highest) * factor)
            total = jnp.sum(expon, axis=1, keepdims=True)
            mixed = jnp.dot(
                expon.astype(jnp.bfloat16), values, preferred_element_type=jnp.float32
            )
            out[first:first + rows, head * HEAD_DIM:(head + 1) * HEAD_DIM] = (
                mixed / total
            ).astype(jnp.bfloat16)


def attend(qkv_rows, frame_ids):
    length, width = qkv_rows.shape
    heads = width // (3 * HEAD_DIM)
    vmem = pl.BlockSpec(memory_space=pltpu.VMEM)
    return pl.pallas_call(
        attend_kernel,
        out_shape=jax.ShapeDtypeStruct((length, heads * HEAD_DIM), jnp.bfloat16),
        in_specs=[vmem] * 3,
        out_specs=vmem,
        compiler_params=pltpu.CompilerParams(vmem_limit_bytes=48 << 20),
        cost_estimate=pl.CostEstimate(
            flops=4 * length * length * HEAD_DIM * heads,
            bytes_accessed=qkv_rows.size * 3,
            transcendentals=length * length * heads,
        ),
    )(frame_ids[:, None], frame_ids[None, :], qkv_rows)


def device_at(section=None, seq=None):
    place = {}
    if section is not None:
        place["section"] = section
    if seq is not None:
        place["seq"] = seq
    return place


def greet(peers):
    barrier = pltpu.get_barrier_semaphore()
    count = 0
    for condition, device in peers:
        if condition is None:
            pl.semaphore_signal(barrier, inc=1, device_id=device, device_id_type=MESH)
            count = count + 1
        else:
            @pl.when(condition)
            def _(device=device):
                pl.semaphore_signal(barrier, inc=1, device_id=device, device_id_type=MESH)

            count = count + condition.astype(jnp.int32)
    pl.semaphore_wait(barrier, count)


def remote(src, dst, send, recv, device):
    return pltpu.make_async_remote_copy(
        src_ref=src, dst_ref=dst, send_sem=send, recv_sem=recv,
        device_id=device, device_id_type=MESH,
    )


def head_kernel(
    sections, line,
    flags, latent, pending, context, w_in, qkv,
    inbox, full, outbox,
    z_send, z_recv, plane_send, plane_recv, sib_send, sib_recv, slab_send, slab_recv,
):
    section = lax.axis_index("section")
    me = lax.axis_index("seq")
    z, core = lax.div(me, 2), lax.rem(me, 2)
    sibling = device_at(seq=2 * z + 1 - core)
    above = device_at(seq=jnp.minimum(me + 2, 2 * line - 1))
    below = device_at(seq=jnp.maximum(me - 2, 0))
    plane = [device_at(section=lax.rem(section + d, sections)) for d in range(1, sections)]
    has_above, has_below = z < line - 1, z > 0
    greet([(None, sibling), (has_above, above), (has_below, below)] + [(None, p) for p in plane])

    pieces, chunk = inbox.shape[1], inbox.shape[3]

    def z_copy(way, block, h):
        return remote(
            inbox.at[block, h], inbox.at[block, h], z_send.at[way, block, h],
            z_recv.at[block, h], above if way == 0 else below,
        )

    for h in range(pieces):
        rows = pl.ds(pl.multiple_of((section * pieces + h) * chunk, chunk), chunk)
        inbox[z, h, 0] = latent[rows, :]
        inbox[z, h, 1] = pending[rows, :]

        @pl.when(has_above)
        def _(h=h):
            z_copy(0, z, h).start()

        @pl.when(has_below)
        def _(h=h):
            z_copy(1, z, h).start()

    def normed(latent_rows, pending_rows, to):
        source = source_of(flags, context, latent_rows, pending_rows, to)
        mean = jnp.mean(source * source, axis=1, keepdims=True)
        return (source * lax.rsqrt(mean + EPSILON)).astype(jnp.bfloat16)

    def own(index, carry):
        q, h = lax.div(index, pieces), lax.rem(index, pieces)
        rows = pl.ds(pl.multiple_of(index * chunk, chunk), chunk)
        full[z, core, q, h] = normed(latent[rows, :], pending[rows, :], section)
        return carry

    lax.fori_loop(0, sections * pieces, own, 0)

    def slab_copy(owner):
        return remote(full.at[z, owner], full.at[z, owner], slab_send, slab_recv, sibling)

    slab_copy(core).start()

    def plane_copy(d, block, h, owner):
        return remote(
            outbox.at[d - 1, block, h], full.at[block, core, owner, h],
            plane_send.at[d - 1, block, h], plane_recv.at[d - 1, block, h], plane[d - 1],
        )

    def sib_copy(block, q, h, owner):
        slot = full.at[block, owner, q, h]
        return remote(slot, slot, sib_send.at[block, q, h], sib_recv.at[block, q, h], sibling)

    def multiply(block):
        rows = full[block].reshape(2 * sections * pieces * chunk, full.shape[-1])
        place = pl.ds(pl.multiple_of(block * rows.shape[0], rows.shape[0]), rows.shape[0])
        for column in range(0, qkv.shape[1], 128):
            qkv[place, column:column + 128] = jnp.dot(
                rows, w_in[:, column:column + 128], preferred_element_type=jnp.float32
            ).astype(jnp.bfloat16)

    def take(block, h, way, onward):
        z_copy(way, block, h).wait_recv()

        @pl.when(onward)
        def _():
            z_copy(way, block, h).start()

        latent_rows, pending_rows = inbox[block, h, 0], inbox[block, h, 1]
        for d in range(1, sections):
            outbox[d - 1, block, h] = normed(
                latent_rows, pending_rows, lax.rem(section + d, sections)
            )
            plane_copy(d, block, h, section).start()
        full[block, core, section, h] = normed(latent_rows, pending_rows, section)
        sib_copy(block, section, h, core).start()

    def pass_on(block, h):
        for d in range(1, sections):
            sender = lax.rem(section + sections - d, sections)
            plane_copy(d, block, h, sender).wait_recv()
            sib_copy(block, sender, h, core).start()

    def finish(block):
        for h in range(pieces):
            for q in range(sections):
                sib_copy(block, q, h, 1 - core).wait_recv()
        multiply(block)

    def step(index, carry):
        k, h = lax.div(index, pieces), lax.rem(index, pieces)

        @pl.when(jnp.logical_and(k < line, z >= k))
        def _():
            take(z - k, h, 0, has_above)

        @pl.when(z + k < line)
        def _():
            take(z + k, h, 1, has_below)

        late = index - 2
        k2, h2 = lax.div(late, pieces), lax.rem(late, pieces)

        @pl.when(jnp.logical_and(k2 >= 1, z >= k2))
        def _():
            pass_on(z - k2, h2)

        @pl.when(jnp.logical_and(k2 >= 1, z + k2 < line))
        def _():
            pass_on(z + k2, h2)

        done = k - 1

        @pl.when(h == 1)
        def _():
            @pl.when(done == 0)
            def _():
                slab_copy(1 - core).wait_recv()
                multiply(z)

            @pl.when(jnp.logical_and(done >= 1, z >= done))
            def _():
                finish(z - done)

            @pl.when(jnp.logical_and(done >= 1, z + done < line))
            def _():
                finish(z + done)

        return carry

    lax.fori_loop(pieces, line * pieces + 2, step, 0)

    slab_copy(core).wait_send()

    def drain(index, carry):
        block, h = lax.div(index, pieces), lax.rem(index, pieces)

        @pl.when(jnp.logical_and(block <= z, has_above))
        def _():
            z_copy(0, block, h).wait_send()

        @pl.when(jnp.logical_and(block >= z, has_below))
        def _():
            z_copy(1, block, h).wait_send()

        @pl.when(block != z)
        def _():
            for d in range(1, sections):
                plane_copy(d, block, h, section).wait_send()
            for q in range(sections):
                sib_copy(block, q, h, core).wait_send()

        return carry

    lax.fori_loop(0, line * pieces, drain, 0)


def head(flags, latent, pending, context, w_in):
    sections, seq = lax.axis_size("section"), lax.axis_size("seq")
    line = seq // 2
    rows, width = latent.shape
    chunk = 16
    pieces = rows // (sections * chunk)
    vmem = pl.BlockSpec(memory_space=pltpu.VMEM)
    smem = pl.BlockSpec(memory_space=pltpu.SMEM)
    dma = pltpu.SemaphoreType.DMA
    bf = jnp.bfloat16
    return pl.pallas_call(
        functools.partial(head_kernel, sections, line),
        out_shape=jax.ShapeDtypeStruct((seq * rows, w_in.shape[1]), bf),
        in_specs=[smem] + [vmem] * 4,
        out_specs=vmem,
        scratch_shapes=[
            pltpu.VMEM((line, pieces, 2, chunk, width), bf),
            pltpu.VMEM((line, 2, sections, pieces, chunk, width), bf),
            pltpu.VMEM((sections - 1, line, pieces, chunk, width), bf),
            dma((2, line, pieces)), dma((line, pieces)),
            dma((sections - 1, line, pieces)), dma((sections - 1, line, pieces)),
            dma((line, sections, pieces)), dma((line, sections, pieces)),
            dma(()), dma(()),
        ],
        compiler_params=pltpu.CompilerParams(
            collective_id=2, has_side_effects=True, vmem_limit_bytes=56 << 20
        ),
        cost_estimate=pl.CostEstimate(
            flops=2 * seq * rows * w_in.size, bytes_accessed=16 << 20, transcendentals=0
        ),
    )(flags, latent, pending, context, w_in)


def source_of(flags, context, latent_rows, pending_rows, to):
    scored = pending_rows.astype(jnp.float32) + flags[1, to] * context[...]
    generator = flags[0, to]
    return generator * latent_rows.astype(jnp.float32) + (1.0 - generator) * scored


def tail_kernel(
    sections, line, finish,
    scale, flags, attn, w2, latent, pending, context, stored,
    block_out, dmd, grad_out,
    attn_sib, w_sib, arrived, leaving, res_out, branch, terms, parts, grads, lines, finals,
    core_send, core_recv, sum_send, sum_recv, plane_send, plane_recv,
    line_send, line_recv, sib_send, sib_recv,
):
    section = lax.axis_index("section")
    me = lax.axis_index("seq")
    z, core = lax.div(me, 2), lax.rem(me, 2)
    sibling = device_at(seq=2 * z + 1 - core)
    above = device_at(seq=jnp.minimum(me + 2, 2 * line - 1))
    below = device_at(seq=jnp.maximum(me - 2, 0))
    plane = [device_at(section=lax.rem(section + d, sections)) for d in range(1, sections)]
    has_above, has_below = z < line - 1, z > 0
    greet([(None, sibling), (has_above, above), (has_below, below)] + [(None, p) for p in plane])

    rows = latent.shape[0]
    both = 2 * rows
    half = w2.shape[2]
    quarter = terms.shape[2]
    tile = 256 if half % 256 == 0 else 128

    w_copy = remote(w2.at[1 - core], w_sib, core_send.at[0], core_recv.at[0], sibling)
    a_copy = remote(attn, attn_sib, core_send.at[1], core_recv.at[1], sibling)
    w_copy.start()
    a_copy.start()
    w_copy.wait()
    a_copy.wait()

    def product(first, amount, column):
        span = pl.ds(pl.multiple_of(first, rows), amount)
        return jnp.dot(
            attn[span, :], w2[core, :, pl.ds(column, tile)], preferred_element_type=jnp.float32
        ) + jnp.dot(
            attn_sib[span, :], w_sib[:, pl.ds(column, tile)], preferred_element_type=jnp.float32
        )

    def sum_copy(way, target):
        return remote(
            leaving.at[target], arrived.at[way, target],
            sum_send.at[way, target], sum_recv.at[way, target],
            above if way == 0 else below,
        )

    def push(way, target, has_before):
        @pl.when(has_before)
        def _():
            sum_copy(way, target).wait_recv()

        for column in range(0, half, tile):
            value = product(target * both, both, column)
            before = arrived[way, target, :, pl.ds(column, tile)].astype(jnp.float32)
            value = value + jnp.where(has_before, before, 0.0)
            leaving[target, :, pl.ds(column, tile)] = value.astype(jnp.bfloat16)
        sum_copy(way, target).start()

    def step(tau, carry):
        @pl.when(tau >= z)
        def _():
            push(0, line - 1 - tau + z, has_below)

        @pl.when(tau >= line - 1 - z)
        def _():
            push(1, tau - (line - 1 - z), has_above)

        return carry

    lax.fori_loop(0, line - 1, step, 0)

    @pl.when(has_below)
    def _():
        sum_copy(0, z).wait_recv()

    @pl.when(has_above)
    def _():
        sum_copy(1, z).wait_recv()

    def own(which, store):
        span = pl.ds(pl.multiple_of(which * rows, rows), rows)
        for column in range(0, half, tile):
            value = product(z * both + which * rows, rows, column)
            up = arrived[0, z, span, pl.ds(column, tile)].astype(jnp.float32)
            down = arrived[1, z, span, pl.ds(column, tile)].astype(jnp.float32)
            store(column, value + jnp.where(has_below, up, 0.0) + jnp.where(has_above, down, 0.0))

    def to_sibling(column, value):
        res_out[:, pl.ds(column, tile)] = value

    def to_branch(column, value):
        branch[core, :, pl.ds(column, tile)] = value

    own(1 - core, to_sibling)
    res_copy = remote(res_out, branch.at[core], core_send.at[2], core_recv.at[2], sibling)
    res_copy.start()
    own(core, to_branch)
    res_copy.wait_send()
    remote(res_out, branch.at[1 - core], core_send.at[2], core_recv.at[2], sibling).wait_recv()

    per_half = half // quarter
    for q in range(sections):
        low = (q % per_half) * quarter
        terms[q] = (scale[0, 0] * branch[q // per_half, :, low:low + quarter]).astype(jnp.bfloat16)

    def plane_copies(phase, src, dst):
        return [
            remote(src(lax.rem(section + d, sections)), dst(d),
                   plane_send.at[phase, d - 1], plane_recv.at[phase, d - 1], plane[d - 1])
            for d in range(1, sections)
        ]

    sends = plane_copies(0, lambda to: terms.at[to], lambda d: parts.at[d - 1])
    for copy in sends:
        copy.start()
    source = source_of(flags, context, latent[...], pending[...], section)
    for h in range(2):
        columns = slice(h * half, (h + 1) * half)
        block_out[:, columns] = (source[:, columns] + branch[h]).astype(jnp.bfloat16)
    total = terms[section].astype(jnp.float32)
    for d in range(1, sections):
        sends[d - 1].wait()
        total = total + parts[d - 1].astype(jnp.float32)
    grad = total.astype(jnp.bfloat16)
    lines[z, core] = grad
    grads[section] = grad

    def line_copy(way, block):
        return remote(
            lines.at[block, core], lines.at[block, core],
            line_send.at[way, block], line_recv.at[way, block], above if way == 0 else below,
        )

    def sib_copy(block):
        return remote(
            lines.at[block, core], lines.at[block, core],
            sib_send.at[block], sib_recv.at[block], sibling,
        )

    @pl.when(has_above)
    def _():
        line_copy(0, z).start()

    @pl.when(has_below)
    def _():
        line_copy(1, z).start()

    sib_copy(z).start()

    def gather(phase, buffer):
        copies = plane_copies(phase, lambda to: buffer.at[section], lambda d: buffer.at[section])
        for copy in copies:
            copy.start()
        return copies

    def gathered(phase, buffer, copies):
        for d in range(1, sections):
            copies[d - 1].wait_send()
            slot = buffer.at[lax.rem(section + sections - d, sections)]
            remote(slot, slot, plane_send.at[phase, d - 1], plane_recv.at[phase, d - 1],
                   plane[d - 1]).wait_recv()

    copies = gather(1, grads)
    for k in range(1, line):
        @pl.when(z >= k)
        def _(k=k):
            line_copy(0, z - k).wait_recv()

            @pl.when(has_above)
            def _():
                line_copy(0, z - k).start()

            sib_copy(z - k).start()

        @pl.when(z + k < line)
        def _(k=k):
            line_copy(1, z + k).wait_recv()

            @pl.when(has_below)
            def _():
                line_copy(1, z + k).start()

            sib_copy(z + k).start()

    def sib_wait(block, carry):
        slot = lines.at[block, 1 - core]
        sib_copy(block).wait_send()
        remote(slot, slot, sib_send.at[block], sib_recv.at[block], sibling).wait_recv()
        return carry

    lax.fori_loop(0, line, sib_wait, 0)
    everything = lines[...].reshape(line * both, quarter)
    local = jnp.dot(stored[...], everything, preferred_element_type=jnp.float32)
    if finish:
        finals[section] = local.astype(jnp.bfloat16)
        last = gather(2, finals)
    else:
        grad_out[...] = local
    gathered(1, grads, copies)
    for q in range(sections):
        dmd[:, q * quarter:(q + 1) * quarter] = grads[q].astype(jnp.float32)

    def line_drain(block, carry):
        @pl.when(jnp.logical_and(block <= z, has_above))
        def _():
            line_copy(0, block).wait_send()

        @pl.when(jnp.logical_and(block >= z, has_below))
        def _():
            line_copy(1, block).wait_send()

        @pl.when(block > z)
        def _():
            sum_copy(0, block).wait_send()

        @pl.when(block < z)
        def _():
            sum_copy(1, block).wait_send()

        return carry

    lax.fori_loop(0, line, line_drain, 0)
    if finish:
        gathered(2, finals, last)
        for q in range(sections):
            grad_out[:, q * quarter:(q + 1) * quarter] = finals[q].astype(jnp.float32)


def tail(scale, flags, attn, w_proj, latent, pending, context, stored, finish):
    sections, seq = lax.axis_size("section"), lax.axis_size("seq")
    line = seq // 2
    rows, width = latent.shape
    length, inner = attn.shape
    half, quarter = width // 2, width // sections
    w2 = w_proj.reshape(inner, 2, half).transpose(1, 0, 2)
    vmem = pl.BlockSpec(memory_space=pltpu.VMEM)
    smem = pl.BlockSpec(memory_space=pltpu.SMEM)
    bf, f32 = jnp.bfloat16, jnp.float32
    dma = pltpu.SemaphoreType.DMA
    return pl.pallas_call(
        functools.partial(tail_kernel, sections, line, finish),
        out_shape=(
            jax.ShapeDtypeStruct((rows, width), bf),
            jax.ShapeDtypeStruct((rows, width), f32),
            jax.ShapeDtypeStruct((inner, width if finish else quarter), f32),
        ),
        in_specs=[smem] * 2 + [vmem] * 6,
        out_specs=(vmem,) * 3,
        scratch_shapes=[
            pltpu.VMEM((length, inner), bf),
            pltpu.VMEM((inner, half), bf),
            pltpu.VMEM((2, line, 2 * rows, half), bf),
            pltpu.VMEM((line, 2 * rows, half), bf),
            pltpu.VMEM((rows, half), f32),
            pltpu.VMEM((2, rows, half), f32),
            pltpu.VMEM((sections, rows, quarter), bf),
            pltpu.VMEM((sections - 1, rows, quarter), bf),
            pltpu.VMEM((sections, rows, quarter), bf),
            pltpu.VMEM((line, 2, rows, quarter), bf),
            pltpu.VMEM((sections, inner, quarter), bf),
            dma((3,)), dma((3,)),
            dma((2, line)), dma((2, line)),
            dma((3, sections - 1)), dma((3, sections - 1)),
            dma((2, line)), dma((2, line)),
            dma((line,)), dma((line,)),
        ],
        compiler_params=pltpu.CompilerParams(
            collective_id=1, has_side_effects=True, vmem_limit_bytes=56 << 20
        ),
        cost_estimate=pl.CostEstimate(
            flops=2 * length * inner * width, bytes_accessed=8 << 20, transcendentals=0
        ),
    )(scale, flags, attn, w2, latent, pending, context, stored)


def per_device(roles, block_ids, latent, pending, context, w_qkv, w_out, stored_attn):
    section = lax.axis_index("section")
    places = jnp.arange(4, dtype=jnp.int32)
    weight_table = jnp.array([0.0, -GUIDE, GUIDE - 1.0, 1.0], jnp.float32)
    section_role = jnp.sum(jnp.where(places == section, roles, 0))
    model_index = jnp.sum(jnp.where(places == section_role, jnp.array([0, 1, 1, 2], jnp.int32), 0))
    score_weight = jnp.sum(jnp.where(places == section_role, weight_table, 0.0))
    w_in = lax.dynamic_index_in_dim(w_qkv, model_index, 0, keepdims=False)
    w_proj = lax.dynamic_index_in_dim(w_out, model_index, 0, keepdims=False)
    is_generator = section_role == 0
    flags = jnp.stack(
        [roles == 0, jnp.logical_or(roles == 1, roles == 3)]
    ).astype(jnp.float32)
    qkv_rows = head(flags, latent[0], pending[0], context, w_in)
    frame_ids = jnp.where(is_generator, block_ids[0, 0], block_ids[1, 0])
    attn = attend(qkv_rows, frame_ids)
    finish = lax.axis_size("dp") == 1
    block_out, gradient, grad_out = tail(
        score_weight.reshape(1, 1), flags, attn, w_proj, latent[0], pending[0], context,
        stored_attn[0].T, finish,
    )
    if not finish:
        grad_out = lax.psum(grad_out, "dp").astype(jnp.bfloat16)
        grad_out = lax.all_gather(grad_out, "section", axis=1, tiled=True).astype(jnp.float32)
    return (block_out[None, None], gradient[None], grad_out)


def solution(mesh):
    placed = (
        P(),
        P(None, "dp", None),
        P("dp", "seq", None),
        P("dp", "seq", None),
        P("dp", None),
        P(None, None, "seq"),
        P(None, "seq", None),
        P("dp", None, "seq"),
    )
    return jax.shard_map(
        per_device,
        mesh=mesh,
        in_specs=placed,
        out_specs=(P("section", "dp", "seq", None), P("dp", "seq", None), P("seq", None)),
        check_vma=False,
    )
```

```python
import functools

import jax
import jax.numpy as jnp
from jax import lax
from jax.experimental import pallas as pl
from jax.experimental.pallas import tpu as pltpu
from jax.sharding import PartitionSpec as P

HEAD_DIM = 128
GUIDE = 3.0
EPSILON = 1e-06
NEGATIVE = -1e30
SPAN_MOST = 384
LOG2E = 1.4426950408889634
MESH = pl.DeviceIdType.MESH


def attend_kernel(ids_col, ids_row, qkv, out):
    length = qkv.shape[0]
    heads = qkv.shape[1] // (3 * HEAD_DIM)
    rows = min(256, length)
    factor = HEAD_DIM ** (-0.5) * LOG2E
    for block in range(length // rows):
        first = block * rows
        seen = min(length, first + rows + SPAN_MOST)
        hidden = ids_row[:, :seen] > ids_col[first:first + rows, :]
        for head in range(heads):
            base = head * 3 * HEAD_DIM
            query = qkv[first:first + rows, base:base + HEAD_DIM]
            keys = qkv[:seen, base + HEAD_DIM:base + 2 * HEAD_DIM]
            values = qkv[:seen, base + 2 * HEAD_DIM:base + 3 * HEAD_DIM]
            scores = lax.dot_general(
                query, keys, (((1,), (1,)), ((), ())), preferred_element_type=jnp.float32
            )
            scores = jnp.where(hidden, NEGATIVE, scores)
            highest = jnp.max(scores, axis=1, keepdims=True)
            expon = jnp.exp2((scores - highest) * factor)
            total = jnp.sum(expon, axis=1, keepdims=True)
            mixed = jnp.dot(
                expon.astype(jnp.bfloat16), values, preferred_element_type=jnp.float32
            )
            out[first:first + rows, head * HEAD_DIM:(head + 1) * HEAD_DIM] = (
                mixed / total
            ).astype(jnp.bfloat16)


def attend(qkv_rows, frame_ids):
    length, width = qkv_rows.shape
    heads = width // (3 * HEAD_DIM)
    vmem = pl.BlockSpec(memory_space=pltpu.VMEM)
    return pl.pallas_call(
        attend_kernel,
        out_shape=jax.ShapeDtypeStruct((length, heads * HEAD_DIM), jnp.bfloat16),
        in_specs=[vmem] * 3,
        out_specs=vmem,
        compiler_params=pltpu.CompilerParams(vmem_limit_bytes=48 << 20),
        cost_estimate=pl.CostEstimate(
            flops=4 * length * length * HEAD_DIM * heads,
            bytes_accessed=qkv_rows.size * 3,
            transcendentals=length * length * heads,
        ),
    )(frame_ids[:, None], frame_ids[None, :], qkv_rows)


def device_at(section=None, seq=None):
    place = {}
    if section is not None:
        place["section"] = section
    if seq is not None:
        place["seq"] = seq
    return place


def greet(peers):
    barrier = pltpu.get_barrier_semaphore()
    count = 0
    for condition, device in peers:
        if condition is None:
            pl.semaphore_signal(barrier, inc=1, device_id=device, device_id_type=MESH)
            count = count + 1
        else:
            @pl.when(condition)
            def _(device=device):
                pl.semaphore_signal(barrier, inc=1, device_id=device, device_id_type=MESH)

            count = count + condition.astype(jnp.int32)
    pl.semaphore_wait(barrier, count)


def remote(src, dst, send, recv, device):
    return pltpu.make_async_remote_copy(
        src_ref=src, dst_ref=dst, send_sem=send, recv_sem=recv,
        device_id=device, device_id_type=MESH,
    )


def head_kernel(
    sections, line,
    flags, latent, pending, context, w_in, qkv,
    inbox, full, outbox,
    z_send, z_recv, plane_send, plane_recv, sib_send, sib_recv, slab_send, slab_recv,
):
    section = lax.axis_index("section")
    me = lax.axis_index("seq")
    z, core = lax.div(me, 2), lax.rem(me, 2)
    sibling = device_at(seq=2 * z + 1 - core)
    above = device_at(seq=jnp.minimum(me + 2, 2 * line - 1))
    below = device_at(seq=jnp.maximum(me - 2, 0))
    plane = [device_at(section=lax.rem(section + d, sections)) for d in range(1, sections)]
    has_above, has_below = z < line - 1, z > 0
    greet([(None, sibling), (has_above, above), (has_below, below)] + [(None, p) for p in plane])

    pieces, chunk = inbox.shape[1], inbox.shape[3]

    def z_copy(way, block, h):
        return remote(
            inbox.at[block, h], inbox.at[block, h], z_send.at[way, block, h],
            z_recv.at[block, h], above if way == 0 else below,
        )

    for h in range(pieces):
        rows = pl.ds(pl.multiple_of((section * pieces + h) * chunk, chunk), chunk)
        inbox[z, h, 0] = latent[rows, :]
        inbox[z, h, 1] = pending[rows, :]

        @pl.when(has_above)
        def _(h=h):
            z_copy(0, z, h).start()

        @pl.when(has_below)
        def _(h=h):
            z_copy(1, z, h).start()

    def normed(latent_rows, pending_rows, to):
        source = source_of(flags, context, latent_rows, pending_rows, to)
        mean = jnp.mean(source * source, axis=1, keepdims=True)
        return (source * lax.rsqrt(mean + EPSILON)).astype(jnp.bfloat16)

    def own(index, carry):
        q, h = lax.div(index, pieces), lax.rem(index, pieces)
        rows = pl.ds(pl.multiple_of(index * chunk, chunk), chunk)
        full[z, core, q, h] = normed(latent[rows, :], pending[rows, :], section)
        return carry

    lax.fori_loop(0, sections * pieces, own, 0)

    def slab_copy(owner):
        return remote(full.at[z, owner], full.at[z, owner], slab_send, slab_recv, sibling)

    slab_copy(core).start()

    def plane_copy(d, block, h, owner):
        return remote(
            outbox.at[d - 1, block, h], full.at[block, core, owner, h],
            plane_send.at[d - 1, block, h], plane_recv.at[d - 1, block, h], plane[d - 1],
        )

    def sib_copy(block, q, h, owner):
        slot = full.at[block, owner, q, h]
        return remote(slot, slot, sib_send.at[block, q, h], sib_recv.at[block, q, h], sibling)

    def multiply(block):
        rows = full[block].reshape(2 * sections * pieces * chunk, full.shape[-1])
        place = pl.ds(pl.multiple_of(block * rows.shape[0], rows.shape[0]), rows.shape[0])
        for column in range(0, qkv.shape[1], 128):
            qkv[place, column:column + 128] = jnp.dot(
                rows, w_in[:, column:column + 128], preferred_element_type=jnp.float32
            ).astype(jnp.bfloat16)

    def take(block, h, way, onward):
        z_copy(way, block, h).wait_recv()

        @pl.when(onward)
        def _():
            z_copy(way, block, h).start()

        latent_rows, pending_rows = inbox[block, h, 0], inbox[block, h, 1]
        for d in range(1, sections):
            outbox[d - 1, block, h] = normed(
                latent_rows, pending_rows, lax.rem(section + d, sections)
            )
            plane_copy(d, block, h, section).start()
        full[block, core, section, h] = normed(latent_rows, pending_rows, section)
        sib_copy(block, section, h, core).start()

    def pass_on(block, h):
        for d in range(1, sections):
            sender = lax.rem(section + sections - d, sections)
            plane_copy(d, block, h, sender).wait_recv()
            sib_copy(block, sender, h, core).start()

    def finish(block):
        for h in range(pieces):
            for q in range(sections):
                sib_copy(block, q, h, 1 - core).wait_recv()
        multiply(block)

    def step(index, carry):
        k, h = lax.div(index, pieces), lax.rem(index, pieces)

        @pl.when(jnp.logical_and(k < line, z >= k))
        def _():
            take(z - k, h, 0, has_above)

        @pl.when(z + k < line)
        def _():
            take(z + k, h, 1, has_below)

        late = index - 2
        k2, h2 = lax.div(late, pieces), lax.rem(late, pieces)

        @pl.when(jnp.logical_and(k2 >= 1, z >= k2))
        def _():
            pass_on(z - k2, h2)

        @pl.when(jnp.logical_and(k2 >= 1, z + k2 < line))
        def _():
            pass_on(z + k2, h2)

        done = k - 1

        @pl.when(h == 1)
        def _():
            @pl.when(done == 0)
            def _():
                slab_copy(1 - core).wait_recv()
                multiply(z)

            @pl.when(jnp.logical_and(done >= 1, z >= done))
            def _():
                finish(z - done)

            @pl.when(jnp.logical_and(done >= 1, z + done < line))
            def _():
                finish(z + done)

        return carry

    lax.fori_loop(pieces, line * pieces + 2, step, 0)

    slab_copy(core).wait_send()

    def drain(index, carry):
        block, h = lax.div(index, pieces), lax.rem(index, pieces)

        @pl.when(jnp.logical_and(block <= z, has_above))
        def _():
            z_copy(0, block, h).wait_send()

        @pl.when(jnp.logical_and(block >= z, has_below))
        def _():
            z_copy(1, block, h).wait_send()

        @pl.when(block != z)
        def _():
            for d in range(1, sections):
                plane_copy(d, block, h, section).wait_send()
            for q in range(sections):
                sib_copy(block, q, h, core).wait_send()

        return carry

    lax.fori_loop(0, line * pieces, drain, 0)


def head(flags, latent, pending, context, w_in):
    sections, seq = lax.axis_size("section"), lax.axis_size("seq")
    line = seq // 2
    rows, width = latent.shape
    chunk = 16
    pieces = rows // (sections * chunk)
    vmem = pl.BlockSpec(memory_space=pltpu.VMEM)
    smem = pl.BlockSpec(memory_space=pltpu.SMEM)
    dma = pltpu.SemaphoreType.DMA
    bf = jnp.bfloat16
    return pl.pallas_call(
        functools.partial(head_kernel, sections, line),
        out_shape=jax.ShapeDtypeStruct((seq * rows, w_in.shape[1]), bf),
        in_specs=[smem] + [vmem] * 4,
        out_specs=vmem,
        scratch_shapes=[
            pltpu.VMEM((line, pieces, 2, chunk, width), bf),
            pltpu.VMEM((line, 2, sections, pieces, chunk, width), bf),
            pltpu.VMEM((sections - 1, line, pieces, chunk, width), bf),
            dma((2, line, pieces)), dma((line, pieces)),
            dma((sections - 1, line, pieces)), dma((sections - 1, line, pieces)),
            dma((line, sections, pieces)), dma((line, sections, pieces)),
            dma(()), dma(()),
        ],
        compiler_params=pltpu.CompilerParams(
            collective_id=2, has_side_effects=True, vmem_limit_bytes=56 << 20
        ),
        cost_estimate=pl.CostEstimate(
            flops=2 * seq * rows * w_in.size, bytes_accessed=16 << 20, transcendentals=0
        ),
    )(flags, latent, pending, context, w_in)


def source_of(flags, context, latent_rows, pending_rows, to):
    scored = pending_rows.astype(jnp.float32) + flags[1, to] * context[...]
    generator = flags[0, to]
    return generator * latent_rows.astype(jnp.float32) + (1.0 - generator) * scored


def tail_kernel(
    sections, line, finish,
    scale, flags, attn, w2, latent, pending, context, stored,
    block_out, dmd, grad_out,
    attn_sib, w_sib, arrived, leaving, res_out, branch, terms, parts, grads, lines, finals,
    core_send, core_recv, sum_send, sum_recv, plane_send, plane_recv,
    line_send, line_recv, sib_send, sib_recv,
):
    section = lax.axis_index("section")
    me = lax.axis_index("seq")
    z, core = lax.div(me, 2), lax.rem(me, 2)
    sibling = device_at(seq=2 * z + 1 - core)
    above = device_at(seq=jnp.minimum(me + 2, 2 * line - 1))
    below = device_at(seq=jnp.maximum(me - 2, 0))
    plane = [device_at(section=lax.rem(section + d, sections)) for d in range(1, sections)]
    has_above, has_below = z < line - 1, z > 0
    greet([(None, sibling), (has_above, above), (has_below, below)] + [(None, p) for p in plane])

    rows = latent.shape[0]
    both = 2 * rows
    half = w2.shape[2]
    quarter = terms.shape[2]
    per_half = half // quarter
    tiles = quarter // 128
    chunks = min(3, tiles)
    edges = [128 * -(-tiles * j // chunks) for j in range(chunks + 1)]
    widths = [edges[j + 1] - edges[j] for j in range(chunks)]

    def lanes(j):
        return slice(edges[j], edges[j + 1])

    def packed(j, part=None):
        if part is None:
            return slice(per_half * edges[j], per_half * edges[j + 1])
        first = per_half * edges[j] + part * widths[j]
        return slice(first, first + widths[j])

    w_copy = remote(w2.at[1 - core], w_sib, core_send.at[0], core_recv.at[0], sibling)
    a_copy = remote(attn, attn_sib, core_send.at[1], core_recv.at[1], sibling)
    w_copy.start()
    a_copy.start()
    w_copy.wait()
    a_copy.wait()

    def product(first, amount, j, part):
        span = pl.ds(pl.multiple_of(first, rows), amount)
        columns = slice(part * quarter + edges[j], part * quarter + edges[j + 1])
        return jnp.dot(
            attn[span, :], w2[core, :, columns], preferred_element_type=jnp.float32
        ) + jnp.dot(
            attn_sib[span, :], w_sib[:, columns], preferred_element_type=jnp.float32
        )

    def sum_copy(j, way, target):
        return remote(
            leaving.at[target, :, packed(j)], arrived.at[way, target, :, packed(j)],
            sum_send.at[j, way, target], sum_recv.at[j, way, target],
            above if way == 0 else below,
        )

    def push(j, way, target, has_before):
        @pl.when(has_before)
        def _():
            sum_copy(j, way, target).wait_recv()

        for part in range(per_half):
            value = product(target * both, both, j, part)
            before = arrived[way, target, :, packed(j, part)].astype(jnp.float32)
            value = value + jnp.where(has_before, before, 0.0)
            leaving[target, :, packed(j, part)] = value.astype(jnp.bfloat16)
        sum_copy(j, way, target).start()

    def pushes(j, first, last):
        def step(tau, carry):
            @pl.when(tau >= z)
            def _():
                push(j, 0, line - 1 - tau + z, has_below)

            @pl.when(tau >= line - 1 - z)
            def _():
                push(j, 1, tau - (line - 1 - z), has_above)

            return carry

        lax.fori_loop(min(first, line - 1), min(last, line - 1), step, 0)

    def res_copy(j, owner):
        return remote(
            res_out.at[:, packed(j)], branch.at[owner, :, packed(j)],
            core_send.at[2 + j], core_recv.at[2 + j], sibling,
        )

    def own_sum(j):
        @pl.when(has_below)
        def _():
            sum_copy(j, 0, z).wait_recv()

        @pl.when(has_above)
        def _():
            sum_copy(j, 1, z).wait_recv()

        def own(which, part):
            span = pl.ds(pl.multiple_of(which * rows, rows), rows)
            value = product(z * both + which * rows, rows, j, part)
            up = arrived[0, z, span, packed(j, part)].astype(jnp.float32)
            down = arrived[1, z, span, packed(j, part)].astype(jnp.float32)
            return value + jnp.where(has_below, up, 0.0) + jnp.where(has_above, down, 0.0)

        for part in range(per_half):
            res_out[:, packed(j, part)] = own(1 - core, part)
        res_copy(j, core).start()
        for part in range(per_half):
            branch[core, :, packed(j, part)] = own(core, part)

    def plane_copies(j, phase, src, dst, which=range(1, sections)):
        return [
            remote(src(lax.rem(section + d, sections)), dst(d),
                   plane_send.at[j, phase, d - 1], plane_recv.at[j, phase, d - 1], plane[d - 1])
            for d in which
        ]

    def term_copies(j):
        return plane_copies(
            j, 0, lambda to: terms.at[to, :, lanes(j)], lambda d: parts.at[d - 1, :, lanes(j)]
        )

    def share(j):
        res_copy(j, core).wait_send()
        res_copy(j, 1 - core).wait_recv()
        for q in range(sections):
            value = branch[q // per_half, :, packed(j, q % per_half)]
            terms[q, :, lanes(j)] = (scale[0, 0] * value).astype(jnp.bfloat16)
        for copy in term_copies(j):
            copy.start()
        for q in range(sections):
            columns = slice(q * quarter + edges[j], q * quarter + edges[j + 1])
            source = source_of(
                flags, context[:, columns], latent[:, columns], pending[:, columns], section
            )
            value = branch[q // per_half, :, packed(j, q % per_half)]
            block_out[:, columns] = (source + value).astype(jnp.bfloat16)

    def line_copy(j, way, block):
        slot = lines.at[block, core, :, lanes(j)]
        return remote(
            slot, slot, line_send.at[j, way, block], line_recv.at[j, way, block],
            above if way == 0 else below,
        )

    def sib_copy(j, block, owner):
        slot = lines.at[block, owner, :, lanes(j)]
        return remote(slot, slot, sib_send.at[j, block], sib_recv.at[j, block], sibling)

    def gather(j, phase, buffer, owner, which=range(1, sections)):
        slot = buffer.at[owner, :, lanes(j)]
        return plane_copies(j, phase, lambda to: slot, lambda d: slot, which)

    def gathered(j, phase, buffer):
        for d in range(1, sections):
            gather(j, phase, buffer, section, [d])[0].wait_send()
            sender = lax.rem(section + sections - d, sections)
            gather(j, phase, buffer, sender, [d])[0].wait_recv()

    def add_up(j):
        total = terms[section, :, lanes(j)].astype(jnp.float32)
        copies = term_copies(j)
        for d in range(1, sections):
            copies[d - 1].wait()
            total = total + parts[d - 1, :, lanes(j)].astype(jnp.float32)
        grad = total.astype(jnp.bfloat16)
        lines[z, core, :, lanes(j)] = grad
        grads[section, :, lanes(j)] = grad

        @pl.when(has_above)
        def _():
            line_copy(j, 0, z).start()

        @pl.when(has_below)
        def _():
            line_copy(j, 1, z).start()

        sib_copy(j, z, core).start()
        for copy in gather(j, 1, grads, section):
            copy.start()

    def spread(j):
        def step(k, carry):
            @pl.when(z >= k)
            def _():
                line_copy(j, 0, z - k).wait_recv()

                @pl.when(has_above)
                def _():
                    line_copy(j, 0, z - k).start()

                sib_copy(j, z - k, core).start()

            @pl.when(z + k < line)
            def _():
                line_copy(j, 1, z + k).wait_recv()

                @pl.when(has_below)
                def _():
                    line_copy(j, 1, z + k).start()

                sib_copy(j, z + k, core).start()

            return carry

        lax.fori_loop(1, line, step, 0)

    def project(j):
        def sib_wait(block, carry):
            sib_copy(j, block, core).wait_send()
            sib_copy(j, block, 1 - core).wait_recv()
            return carry

        lax.fori_loop(0, line, sib_wait, 0)
        everything = lines[:, :, :, lanes(j)].reshape(line * both, widths[j])
        local = jnp.dot(stored[...], everything, preferred_element_type=jnp.float32)
        if finish:
            finals[section, :, lanes(j)] = local.astype(jnp.bfloat16)
            for copy in gather(j, 2, finals, section):
                copy.start()
        else:
            grad_out[:, lanes(j)] = local

    pushes(0, 0, line)
    for j in range(chunks):
        if j + 1 < chunks:
            pushes(j + 1, 0, 1)
        own_sum(j)
        if j + 1 < chunks:
            pushes(j + 1, 1, 2)
        share(j)
        if j >= 1:
            spread(j - 1)
        if j + 1 < chunks:
            pushes(j + 1, 2, line)
        add_up(j)
        if j >= 1:
            project(j - 1)
    spread(chunks - 1)
    project(chunks - 1)

    for j in range(chunks):
        gathered(j, 1, grads)
        for q in range(sections):
            columns = slice(q * quarter + edges[j], q * quarter + edges[j + 1])
            dmd[:, columns] = grads[q, :, lanes(j)].astype(jnp.float32)

    def line_drain(block, carry):
        for j in range(chunks):
            @pl.when(jnp.logical_and(block <= z, has_above))
            def _(j=j):
                line_copy(j, 0, block).wait_send()

            @pl.when(jnp.logical_and(block >= z, has_below))
            def _(j=j):
                line_copy(j, 1, block).wait_send()

            @pl.when(block > z)
            def _(j=j):
                sum_copy(j, 0, block).wait_send()

            @pl.when(block < z)
            def _(j=j):
                sum_copy(j, 1, block).wait_send()

        return carry

    lax.fori_loop(0, line, line_drain, 0)
    if finish:
        for j in range(chunks):
            gathered(j, 2, finals)
            for q in range(sections):
                columns = slice(q * quarter + edges[j], q * quarter + edges[j + 1])
                grad_out[:, columns] = finals[q, :, lanes(j)].astype(jnp.float32)


def tail(scale, flags, attn, w_proj, latent, pending, context, stored, finish):
    sections, seq = lax.axis_size("section"), lax.axis_size("seq")
    line = seq // 2
    rows, width = latent.shape
    length, inner = attn.shape
    half, quarter = width // 2, width // sections
    w2 = w_proj.reshape(inner, 2, half).transpose(1, 0, 2)
    vmem = pl.BlockSpec(memory_space=pltpu.VMEM)
    smem = pl.BlockSpec(memory_space=pltpu.SMEM)
    bf, f32 = jnp.bfloat16, jnp.float32
    dma = pltpu.SemaphoreType.DMA
    return pl.pallas_call(
        functools.partial(tail_kernel, sections, line, finish),
        out_shape=(
            jax.ShapeDtypeStruct((rows, width), bf),
            jax.ShapeDtypeStruct((rows, width), f32),
            jax.ShapeDtypeStruct((inner, width if finish else quarter), f32),
        ),
        in_specs=[smem] * 2 + [vmem] * 6,
        out_specs=(vmem,) * 3,
        scratch_shapes=[
            pltpu.VMEM((length, inner), bf),
            pltpu.VMEM((inner, half), bf),
            pltpu.VMEM((2, line, 2 * rows, half), bf),
            pltpu.VMEM((line, 2 * rows, half), bf),
            pltpu.VMEM((rows, half), f32),
            pltpu.VMEM((2, rows, half), f32),
            pltpu.VMEM((sections, rows, quarter), bf),
            pltpu.VMEM((sections - 1, rows, quarter), bf),
            pltpu.VMEM((sections, rows, quarter), bf),
            pltpu.VMEM((line, 2, rows, quarter), bf),
            pltpu.VMEM((sections, inner, quarter), bf),
            dma((5,)), dma((5,)),
            dma((3, 2, line)), dma((3, 2, line)),
            dma((3, 3, sections - 1)), dma((3, 3, sections - 1)),
            dma((3, 2, line)), dma((3, 2, line)),
            dma((3, line)), dma((3, line)),
        ],
        compiler_params=pltpu.CompilerParams(
            collective_id=1, has_side_effects=True, vmem_limit_bytes=56 << 20
        ),
        cost_estimate=pl.CostEstimate(
            flops=2 * length * inner * width, bytes_accessed=8 << 20, transcendentals=0
        ),
    )(scale, flags, attn, w2, latent, pending, context, stored)


def per_device(roles, block_ids, latent, pending, context, w_qkv, w_out, stored_attn):
    section = lax.axis_index("section")
    places = jnp.arange(4, dtype=jnp.int32)
    weight_table = jnp.array([0.0, -GUIDE, GUIDE - 1.0, 1.0], jnp.float32)
    section_role = jnp.sum(jnp.where(places == section, roles, 0))
    model_index = jnp.sum(jnp.where(places == section_role, jnp.array([0, 1, 1, 2], jnp.int32), 0))
    score_weight = jnp.sum(jnp.where(places == section_role, weight_table, 0.0))
    w_in = lax.dynamic_index_in_dim(w_qkv, model_index, 0, keepdims=False)
    w_proj = lax.dynamic_index_in_dim(w_out, model_index, 0, keepdims=False)
    is_generator = section_role == 0
    flags = jnp.stack(
        [roles == 0, jnp.logical_or(roles == 1, roles == 3)]
    ).astype(jnp.float32)
    qkv_rows = head(flags, latent[0], pending[0], context, w_in)
    frame_ids = jnp.where(is_generator, block_ids[0, 0], block_ids[1, 0])
    attn = attend(qkv_rows, frame_ids)
    finish = lax.axis_size("dp") == 1
    block_out, gradient, grad_out = tail(
        score_weight.reshape(1, 1), flags, attn, w_proj, latent[0], pending[0], context,
        stored_attn[0].T, finish,
    )
    if not finish:
        grad_out = lax.psum(grad_out, "dp").astype(jnp.bfloat16)
        grad_out = lax.all_gather(grad_out, "section", axis=1, tiled=True).astype(jnp.float32)
    return (block_out[None, None], gradient[None], grad_out)


def solution(mesh):
    placed = (
        P(),
        P(None, "dp", None),
        P("dp", "seq", None),
        P("dp", "seq", None),
        P("dp", None),
        P(None, None, "seq"),
        P(None, "seq", None),
        P("dp", None, "seq"),
    )
    return jax.shard_map(
        per_device,
        mesh=mesh,
        in_specs=placed,
        out_specs=(P("section", "dp", "seq", None), P("dp", "seq", None), P("seq", None)),
        check_vma=False,
    )
```

```python
import functools

import jax
import jax.numpy as jnp
from jax import lax
from jax.experimental import pallas as pl
from jax.experimental.pallas import tpu as pltpu
from jax.sharding import PartitionSpec as P

HEAD_DIM = 128
GUIDE = 3.0
EPSILON = 1e-06
NEGATIVE = -1e30
SPAN_MOST = 384
LOG2E = 1.4426950408889634
MESH = pl.DeviceIdType.MESH


def attend_kernel(ids_col, ids_row, qkv, out):
    length = qkv.shape[0]
    heads = qkv.shape[1] // (3 * HEAD_DIM)
    rows = min(256, length)
    factor = HEAD_DIM ** (-0.5) * LOG2E
    for block in range(length // rows):
        first = block * rows
        seen = min(length, first + rows + SPAN_MOST)
        hidden = ids_row[:, :seen] > ids_col[first:first + rows, :]
        for head in range(heads):
            base = head * 3 * HEAD_DIM
            query = qkv[first:first + rows, base:base + HEAD_DIM]
            keys = qkv[:seen, base + HEAD_DIM:base + 2 * HEAD_DIM]
            values = qkv[:seen, base + 2 * HEAD_DIM:base + 3 * HEAD_DIM]
            scores = lax.dot_general(
                query, keys, (((1,), (1,)), ((), ())), preferred_element_type=jnp.float32
            )
            scores = jnp.where(hidden, NEGATIVE, scores)
            highest = jnp.max(scores, axis=1, keepdims=True)
            expon = jnp.exp2((scores - highest) * factor)
            total = jnp.sum(expon, axis=1, keepdims=True)
            mixed = jnp.dot(
                expon.astype(jnp.bfloat16), values, preferred_element_type=jnp.float32
            )
            out[first:first + rows, head * HEAD_DIM:(head + 1) * HEAD_DIM] = (
                mixed / total
            ).astype(jnp.bfloat16)


def attend(qkv_rows, frame_ids):
    length, width = qkv_rows.shape
    heads = width // (3 * HEAD_DIM)
    vmem = pl.BlockSpec(memory_space=pltpu.VMEM)
    return pl.pallas_call(
        attend_kernel,
        out_shape=jax.ShapeDtypeStruct((length, heads * HEAD_DIM), jnp.bfloat16),
        in_specs=[vmem] * 3,
        out_specs=vmem,
        compiler_params=pltpu.CompilerParams(vmem_limit_bytes=48 << 20),
        cost_estimate=pl.CostEstimate(
            flops=4 * length * length * HEAD_DIM * heads,
            bytes_accessed=qkv_rows.size * 3,
            transcendentals=length * length * heads,
        ),
    )(frame_ids[:, None], frame_ids[None, :], qkv_rows)


def device_at(section=None, seq=None):
    place = {}
    if section is not None:
        place["section"] = section
    if seq is not None:
        place["seq"] = seq
    return place


def greet(peers):
    barrier = pltpu.get_barrier_semaphore()
    count = 0
    for condition, device in peers:
        if condition is None:
            pl.semaphore_signal(barrier, inc=1, device_id=device, device_id_type=MESH)
            count = count + 1
        else:
            @pl.when(condition)
            def _(device=device):
                pl.semaphore_signal(barrier, inc=1, device_id=device, device_id_type=MESH)

            count = count + condition.astype(jnp.int32)
    pl.semaphore_wait(barrier, count)


def remote(src, dst, send, recv, device):
    return pltpu.make_async_remote_copy(
        src_ref=src, dst_ref=dst, send_sem=send, recv_sem=recv,
        device_id=device, device_id_type=MESH,
    )


def head_kernel(
    sections, line,
    flags, latent, pending, context, w_qkv, w_out, qkv, w_proj,
    inbox, full, outbox, w_all, o_all, w_in,
    z_send, z_recv, plane_send, plane_recv, sib_send, sib_recv, slab_send, slab_recv, load,
):
    section = lax.axis_index("section")
    me = lax.axis_index("seq")
    z, core = lax.div(me, 2), lax.rem(me, 2)
    sibling = device_at(seq=2 * z + 1 - core)
    above = device_at(seq=jnp.minimum(me + 2, 2 * line - 1))
    below = device_at(seq=jnp.maximum(me - 2, 0))
    plane = [device_at(section=lax.rem(section + d, sections)) for d in range(1, sections)]
    has_above, has_below = z < line - 1, z > 0
    greet([(None, sibling), (has_above, above), (has_below, below)] + [(None, p) for p in plane])

    pieces, chunk = inbox.shape[1], inbox.shape[3]
    loads = [
        pltpu.make_async_copy(w_qkv, w_all, load.at[0]),
        pltpu.make_async_copy(w_out, o_all, load.at[1]),
    ]
    for copy in loads:
        copy.start()

    def z_copy(way, block, h):
        return remote(
            inbox.at[block, h], inbox.at[block, h], z_send.at[way, block, h],
            z_recv.at[block, h], above if way == 0 else below,
        )

    for h in range(pieces):
        rows = pl.ds(pl.multiple_of((section * pieces + h) * chunk, chunk), chunk)
        inbox[z, h, 0] = latent[rows, :]
        inbox[z, h, 1] = pending[rows, :]

        @pl.when(has_above)
        def _(h=h):
            z_copy(0, z, h).start()

        @pl.when(has_below)
        def _(h=h):
            z_copy(1, z, h).start()

    def normed(latent_rows, pending_rows, to):
        source = source_of(flags, context, latent_rows, pending_rows, to)
        mean = jnp.mean(source * source, axis=1, keepdims=True)
        return (source * lax.rsqrt(mean + EPSILON)).astype(jnp.bfloat16)

    def own(index, carry):
        q, h = lax.div(index, pieces), lax.rem(index, pieces)
        rows = pl.ds(pl.multiple_of(index * chunk, chunk), chunk)
        full[z, core, q, h] = normed(latent[rows, :], pending[rows, :], section)
        return carry

    lax.fori_loop(0, sections * pieces, own, 0)

    def slab_copy(owner):
        return remote(full.at[z, owner], full.at[z, owner], slab_send, slab_recv, sibling)

    slab_copy(core).start()

    for copy, every, chosen in zip(loads, (w_all, o_all), (w_in, w_proj)):
        copy.wait()
        amount = min(128, chosen.shape[0])

        def choose(index, carry, every=every, chosen=chosen, amount=amount):
            rows = pl.ds(pl.multiple_of(index * amount, amount), amount)
            last = jnp.where(flags[2, 1] > 0.5, every[1, rows, :], every[2, rows, :])
            chosen[rows, :] = jnp.where(flags[2, 0] > 0.5, every[0, rows, :], last)
            return carry

        lax.fori_loop(0, chosen.shape[0] // amount, choose, 0)

    def plane_copy(d, block, h, owner):
        return remote(
            outbox.at[d - 1, block, h], full.at[block, core, owner, h],
            plane_send.at[d - 1, block, h], plane_recv.at[d - 1, block, h], plane[d - 1],
        )

    def sib_copy(block, q, h, owner):
        slot = full.at[block, owner, q, h]
        return remote(slot, slot, sib_send.at[block, q, h], sib_recv.at[block, q, h], sibling)

    def multiply(block):
        rows = full[block].reshape(2 * sections * pieces * chunk, full.shape[-1])
        place = pl.ds(pl.multiple_of(block * rows.shape[0], rows.shape[0]), rows.shape[0])
        for column in range(0, qkv.shape[1], 128):
            qkv[place, column:column + 128] = jnp.dot(
                rows, w_in[:, column:column + 128], preferred_element_type=jnp.float32
            ).astype(jnp.bfloat16)

    def take(block, h, way, onward):
        z_copy(way, block, h).wait_recv()

        @pl.when(onward)
        def _():
            z_copy(way, block, h).start()

        latent_rows, pending_rows = inbox[block, h, 0], inbox[block, h, 1]
        for d in range(1, sections):
            outbox[d - 1, block, h] = normed(
                latent_rows, pending_rows, lax.rem(section + d, sections)
            )
            plane_copy(d, block, h, section).start()
        full[block, core, section, h] = normed(latent_rows, pending_rows, section)
        sib_copy(block, section, h, core).start()

    def pass_on(block, h):
        for d in range(1, sections):
            sender = lax.rem(section + sections - d, sections)
            plane_copy(d, block, h, sender).wait_recv()
            sib_copy(block, sender, h, core).start()

    def finish(block):
        for h in range(pieces):
            for q in range(sections):
                sib_copy(block, q, h, 1 - core).wait_recv()
        multiply(block)

    def step(index, carry):
        k, h = lax.div(index, pieces), lax.rem(index, pieces)

        @pl.when(jnp.logical_and(k < line, z >= k))
        def _():
            take(z - k, h, 0, has_above)

        @pl.when(z + k < line)
        def _():
            take(z + k, h, 1, has_below)

        late = index - 2
        k2, h2 = lax.div(late, pieces), lax.rem(late, pieces)

        @pl.when(jnp.logical_and(k2 >= 1, z >= k2))
        def _():
            pass_on(z - k2, h2)

        @pl.when(jnp.logical_and(k2 >= 1, z + k2 < line))
        def _():
            pass_on(z + k2, h2)

        done = k - 1

        @pl.when(h == 1)
        def _():
            @pl.when(done == 0)
            def _():
                slab_copy(1 - core).wait_recv()
                multiply(z)

            @pl.when(jnp.logical_and(done >= 1, z >= done))
            def _():
                finish(z - done)

            @pl.when(jnp.logical_and(done >= 1, z + done < line))
            def _():
                finish(z + done)

        return carry

    lax.fori_loop(pieces, line * pieces + 2, step, 0)

    slab_copy(core).wait_send()

    def drain(index, carry):
        block, h = lax.div(index, pieces), lax.rem(index, pieces)

        @pl.when(jnp.logical_and(block <= z, has_above))
        def _():
            z_copy(0, block, h).wait_send()

        @pl.when(jnp.logical_and(block >= z, has_below))
        def _():
            z_copy(1, block, h).wait_send()

        @pl.when(block != z)
        def _():
            for d in range(1, sections):
                plane_copy(d, block, h, section).wait_send()
            for q in range(sections):
                sib_copy(block, q, h, core).wait_send()

        return carry

    lax.fori_loop(0, line * pieces, drain, 0)


def head(flags, latent, pending, context, w_qkv, w_out):
    sections, seq = lax.axis_size("section"), lax.axis_size("seq")
    line = seq // 2
    rows, width = latent.shape
    chunk = 16
    pieces = rows // (sections * chunk)
    vmem = pl.BlockSpec(memory_space=pltpu.VMEM)
    smem = pl.BlockSpec(memory_space=pltpu.SMEM)
    dma = pltpu.SemaphoreType.DMA
    bf = jnp.bfloat16
    return pl.pallas_call(
        functools.partial(head_kernel, sections, line),
        out_shape=(
            jax.ShapeDtypeStruct((seq * rows, w_qkv.shape[2]), bf),
            jax.ShapeDtypeStruct(w_out.shape[1:], bf),
        ),
        in_specs=[smem] + [vmem] * 3 + [pl.BlockSpec(memory_space=pl.ANY)] * 2,
        out_specs=(vmem, vmem),
        scratch_shapes=[
            pltpu.VMEM((line, pieces, 2, chunk, width), bf),
            pltpu.VMEM((line, 2, sections, pieces, chunk, width), bf),
            pltpu.VMEM((sections - 1, line, pieces, chunk, width), bf),
            pltpu.VMEM(w_qkv.shape, bf),
            pltpu.VMEM(w_out.shape, bf),
            pltpu.VMEM(w_qkv.shape[1:], bf),
            dma((2, line, pieces)), dma((line, pieces)),
            dma((sections - 1, line, pieces)), dma((sections - 1, line, pieces)),
            dma((line, sections, pieces)), dma((line, sections, pieces)),
            dma(()), dma(()), dma((2,)),
        ],
        compiler_params=pltpu.CompilerParams(
            collective_id=2, has_side_effects=True, vmem_limit_bytes=56 << 20
        ),
        cost_estimate=pl.CostEstimate(
            flops=2 * seq * rows * w_qkv.size // w_qkv.shape[0], bytes_accessed=16 << 20, transcendentals=0
        ),
    )(flags, latent, pending, context, w_qkv, w_out)


def source_of(flags, context, latent_rows, pending_rows, to):
    scored = pending_rows.astype(jnp.float32) + flags[1, to] * context[...]
    generator = flags[0, to]
    return generator * latent_rows.astype(jnp.float32) + (1.0 - generator) * scored


def tail_kernel(
    sections, line, finish,
    scale, flags, attn, w2, latent, pending, context, stored,
    block_out, dmd, grad_out,
    attn_sib, w_sib, arrived, leaving, res_out, branch, terms, parts, grads, lines, finals, stored_t,
    core_send, core_recv, sum_send, sum_recv, plane_send, plane_recv,
    line_send, line_recv, sib_send, sib_recv,
):
    section = lax.axis_index("section")
    me = lax.axis_index("seq")
    z, core = lax.div(me, 2), lax.rem(me, 2)
    sibling = device_at(seq=2 * z + 1 - core)
    above = device_at(seq=jnp.minimum(me + 2, 2 * line - 1))
    below = device_at(seq=jnp.maximum(me - 2, 0))
    plane = [device_at(section=lax.rem(section + d, sections)) for d in range(1, sections)]
    has_above, has_below = z < line - 1, z > 0
    greet([(None, sibling), (has_above, above), (has_below, below)] + [(None, p) for p in plane])

    rows = latent.shape[0]
    both = 2 * rows
    half = w2.shape[1] // 2
    quarter = terms.shape[2]
    per_half = half // quarter
    tiles = quarter // 128
    chunks = min(3, tiles)
    edges = [128 * -(-tiles * j // chunks) for j in range(chunks + 1)]
    widths = [edges[j + 1] - edges[j] for j in range(chunks)]

    def lanes(j):
        return slice(edges[j], edges[j + 1])

    def packed(j, part=None):
        if part is None:
            return slice(per_half * edges[j], per_half * edges[j + 1])
        first = per_half * edges[j] + part * widths[j]
        return slice(first, first + widths[j])

    w_copy = remote(
        w2.at[:, pl.ds(pl.multiple_of((1 - core) * half, 128), half)], w_sib,
        core_send.at[0], core_recv.at[0], sibling)
    a_copy = remote(attn, attn_sib, core_send.at[1], core_recv.at[1], sibling)
    w_copy.start()
    a_copy.start()
    w_copy.wait()
    a_copy.wait()

    def product(first, amount, j, part):
        span = pl.ds(pl.multiple_of(first, rows), amount)
        columns = slice(part * quarter + edges[j], part * quarter + edges[j + 1])
        mine = pl.ds(pl.multiple_of(core * half + columns.start, 128), widths[j])
        return jnp.dot(
            attn[span, :], w2[:, mine], preferred_element_type=jnp.float32
        ) + jnp.dot(
            attn_sib[span, :], w_sib[:, columns], preferred_element_type=jnp.float32
        )

    def sum_copy(j, way, target):
        return remote(
            leaving.at[target, :, packed(j)], arrived.at[way, target, :, packed(j)],
            sum_send.at[j, way, target], sum_recv.at[j, way, target],
            above if way == 0 else below,
        )

    def push(j, way, target, has_before):
        @pl.when(has_before)
        def _():
            sum_copy(j, way, target).wait_recv()

        for part in range(per_half):
            value = product(target * both, both, j, part)
            before = arrived[way, target, :, packed(j, part)].astype(jnp.float32)
            value = value + jnp.where(has_before, before, 0.0)
            leaving[target, :, packed(j, part)] = value.astype(jnp.bfloat16)
        sum_copy(j, way, target).start()

    def pushes(j, first, last):
        def step(tau, carry):
            @pl.when(tau >= z)
            def _():
                push(j, 0, line - 1 - tau + z, has_below)

            @pl.when(tau >= line - 1 - z)
            def _():
                push(j, 1, tau - (line - 1 - z), has_above)

            return carry

        lax.fori_loop(min(first, line - 1), min(last, line - 1), step, 0)

    def res_copy(j, owner):
        return remote(
            res_out.at[:, packed(j)], branch.at[owner, :, packed(j)],
            core_send.at[2 + j], core_recv.at[2 + j], sibling,
        )

    def own_sum(j):
        @pl.when(has_below)
        def _():
            sum_copy(j, 0, z).wait_recv()

        @pl.when(has_above)
        def _():
            sum_copy(j, 1, z).wait_recv()

        def own(which, part):
            span = pl.ds(pl.multiple_of(which * rows, rows), rows)
            value = product(z * both + which * rows, rows, j, part)
            up = arrived[0, z, span, packed(j, part)].astype(jnp.float32)
            down = arrived[1, z, span, packed(j, part)].astype(jnp.float32)
            return value + jnp.where(has_below, up, 0.0) + jnp.where(has_above, down, 0.0)

        for part in range(per_half):
            res_out[:, packed(j, part)] = own(1 - core, part)
        res_copy(j, core).start()
        for part in range(per_half):
            branch[core, :, packed(j, part)] = own(core, part)

    def plane_copies(j, phase, src, dst, which=range(1, sections)):
        return [
            remote(src(lax.rem(section + d, sections)), dst(d),
                   plane_send.at[j, phase, d - 1], plane_recv.at[j, phase, d - 1], plane[d - 1])
            for d in which
        ]

    def term_copies(j):
        return plane_copies(
            j, 0, lambda to: terms.at[to, :, lanes(j)], lambda d: parts.at[d - 1, :, lanes(j)]
        )

    def share(j):
        res_copy(j, core).wait_send()
        res_copy(j, 1 - core).wait_recv()
        for q in range(sections):
            value = branch[q // per_half, :, packed(j, q % per_half)]
            terms[q, :, lanes(j)] = (scale[0, 0] * value).astype(jnp.bfloat16)
        for copy in term_copies(j):
            copy.start()
        for q in range(sections):
            columns = slice(q * quarter + edges[j], q * quarter + edges[j + 1])
            source = source_of(
                flags, context[:, columns], latent[:, columns], pending[:, columns], section
            )
            value = branch[q // per_half, :, packed(j, q % per_half)]
            block_out[:, columns] = (source + value).astype(jnp.bfloat16)

    def line_copy(j, way, block):
        slot = lines.at[block, core, :, lanes(j)]
        return remote(
            slot, slot, line_send.at[j, way, block], line_recv.at[j, way, block],
            above if way == 0 else below,
        )

    def sib_copy(j, block, owner):
        slot = lines.at[block, owner, :, lanes(j)]
        return remote(slot, slot, sib_send.at[j, block], sib_recv.at[j, block], sibling)

    def gather(j, phase, buffer, owner, which=range(1, sections)):
        slot = buffer.at[owner, :, lanes(j)]
        return plane_copies(j, phase, lambda to: slot, lambda d: slot, which)

    def gathered(j, phase, buffer):
        for d in range(1, sections):
            gather(j, phase, buffer, section, [d])[0].wait_send()
            sender = lax.rem(section + sections - d, sections)
            gather(j, phase, buffer, sender, [d])[0].wait_recv()

    def add_up(j):
        total = terms[section, :, lanes(j)].astype(jnp.float32)
        copies = term_copies(j)
        for d in range(1, sections):
            copies[d - 1].wait()
            total = total + parts[d - 1, :, lanes(j)].astype(jnp.float32)
        grad = total.astype(jnp.bfloat16)
        lines[z, core, :, lanes(j)] = grad
        grads[section, :, lanes(j)] = grad

        @pl.when(has_above)
        def _():
            line_copy(j, 0, z).start()

        @pl.when(has_below)
        def _():
            line_copy(j, 1, z).start()

        sib_copy(j, z, core).start()
        for copy in gather(j, 1, grads, section):
            copy.start()

    def spread(j):
        def step(k, carry):
            @pl.when(z >= k)
            def _():
                line_copy(j, 0, z - k).wait_recv()

                @pl.when(has_above)
                def _():
                    line_copy(j, 0, z - k).start()

                sib_copy(j, z - k, core).start()

            @pl.when(z + k < line)
            def _():
                line_copy(j, 1, z + k).wait_recv()

                @pl.when(has_below)
                def _():
                    line_copy(j, 1, z + k).start()

                sib_copy(j, z + k, core).start()

            return carry

        lax.fori_loop(1, line, step, 0)

    def project(j):
        def sib_wait(block, carry):
            sib_copy(j, block, core).wait_send()
            sib_copy(j, block, 1 - core).wait_recv()
            return carry

        lax.fori_loop(0, line, sib_wait, 0)
        everything = lines[:, :, :, lanes(j)].reshape(line * both, widths[j])
        local = jnp.dot(stored_t[...], everything, preferred_element_type=jnp.float32)
        if finish:
            finals[section, :, lanes(j)] = local.astype(jnp.bfloat16)
            for copy in gather(j, 2, finals, section):
                copy.start()
        else:
            grad_out[:, lanes(j)] = local

    pushes(0, 0, line)
    stored_t[...] = stored[...].T
    for j in range(chunks):
        if j + 1 < chunks:
            pushes(j + 1, 0, 1)
        own_sum(j)
        if j + 1 < chunks:
            pushes(j + 1, 1, 2)
        share(j)
        if j >= 1:
            spread(j - 1)
        if j + 1 < chunks:
            pushes(j + 1, 2, line)
        add_up(j)
        if j >= 1:
            project(j - 1)
    spread(chunks - 1)
    project(chunks - 1)

    for j in range(chunks):
        gathered(j, 1, grads)
        for q in range(sections):
            columns = slice(q * quarter + edges[j], q * quarter + edges[j + 1])
            dmd[:, columns] = grads[q, :, lanes(j)].astype(jnp.float32)

    def line_drain(block, carry):
        for j in range(chunks):
            @pl.when(jnp.logical_and(block <= z, has_above))
            def _(j=j):
                line_copy(j, 0, block).wait_send()

            @pl.when(jnp.logical_and(block >= z, has_below))
            def _(j=j):
                line_copy(j, 1, block).wait_send()

            @pl.when(block > z)
            def _(j=j):
                sum_copy(j, 0, block).wait_send()

            @pl.when(block < z)
            def _(j=j):
                sum_copy(j, 1, block).wait_send()

        return carry

    lax.fori_loop(0, line, line_drain, 0)
    if finish:
        for j in range(chunks):
            gathered(j, 2, finals)
            for q in range(sections):
                columns = slice(q * quarter + edges[j], q * quarter + edges[j + 1])
                grad_out[:, columns] = finals[q, :, lanes(j)].astype(jnp.float32)


def tail(scale, flags, attn, w_proj, latent, pending, context, stored, finish):
    sections, seq = lax.axis_size("section"), lax.axis_size("seq")
    line = seq // 2
    rows, width = latent.shape
    length, inner = attn.shape
    half, quarter = width // 2, width // sections
    vmem = pl.BlockSpec(memory_space=pltpu.VMEM)
    smem = pl.BlockSpec(memory_space=pltpu.SMEM)
    bf, f32 = jnp.bfloat16, jnp.float32
    dma = pltpu.SemaphoreType.DMA
    return pl.pallas_call(
        functools.partial(tail_kernel, sections, line, finish),
        out_shape=(
            jax.ShapeDtypeStruct((rows, width), bf),
            jax.ShapeDtypeStruct((rows, width), f32),
            jax.ShapeDtypeStruct((inner, width if finish else quarter), f32),
        ),
        in_specs=[smem] * 2 + [vmem] * 6,
        out_specs=(vmem,) * 3,
        scratch_shapes=[
            pltpu.VMEM((length, inner), bf),
            pltpu.VMEM((inner, half), bf),
            pltpu.VMEM((2, line, 2 * rows, half), bf),
            pltpu.VMEM((line, 2 * rows, half), bf),
            pltpu.VMEM((rows, half), f32),
            pltpu.VMEM((2, rows, half), f32),
            pltpu.VMEM((sections, rows, quarter), bf),
            pltpu.VMEM((sections - 1, rows, quarter), bf),
            pltpu.VMEM((sections, rows, quarter), bf),
            pltpu.VMEM((line, 2, rows, quarter), bf),
            pltpu.VMEM((sections, inner, quarter), bf),
            pltpu.VMEM((inner, length), bf),
            dma((5,)), dma((5,)),
            dma((3, 2, line)), dma((3, 2, line)),
            dma((3, 3, sections - 1)), dma((3, 3, sections - 1)),
            dma((3, 2, line)), dma((3, 2, line)),
            dma((3, line)), dma((3, line)),
        ],
        compiler_params=pltpu.CompilerParams(
            collective_id=1, has_side_effects=True, vmem_limit_bytes=56 << 20
        ),
        cost_estimate=pl.CostEstimate(
            flops=2 * length * inner * width, bytes_accessed=8 << 20, transcendentals=0
        ),
    )(scale, flags, attn, w_proj, latent, pending, context, stored)


def per_device(roles, block_ids, latent, pending, context, w_qkv, w_out, stored_attn):
    section = lax.axis_index("section")
    places = jnp.arange(4, dtype=jnp.int32)
    weight_table = jnp.array([0.0, -GUIDE, GUIDE - 1.0, 1.0], jnp.float32)
    section_role = jnp.sum(jnp.where(places == section, roles, 0))
    model_index = jnp.sum(jnp.where(places == section_role, jnp.array([0, 1, 1, 2], jnp.int32), 0))
    score_weight = jnp.sum(jnp.where(places == section_role, weight_table, 0.0))
    is_generator = section_role == 0
    flags = jnp.stack(
        [roles == 0, jnp.logical_or(roles == 1, roles == 3), places == model_index]
    ).astype(jnp.float32)
    qkv_rows, w_proj = head(flags, latent[0], pending[0], context, w_qkv, w_out)
    frame_ids = jnp.where(is_generator, block_ids[0, 0], block_ids[1, 0])
    attn = attend(qkv_rows, frame_ids)
    finish = lax.axis_size("dp") == 1
    block_out, gradient, grad_out = tail(
        score_weight.reshape(1, 1), flags, attn, w_proj, latent[0], pending[0], context,
        stored_attn[0], finish,
    )
    if not finish:
        grad_out = lax.psum(grad_out, "dp").astype(jnp.bfloat16)
        grad_out = lax.all_gather(grad_out, "section", axis=1, tiled=True).astype(jnp.float32)
    return (block_out[None, None], gradient[None], grad_out)


def solution(mesh):
    placed = (
        P(),
        P(None, "dp", None),
        P("dp", "seq", None),
        P("dp", "seq", None),
        P("dp", None),
        P(None, None, "seq"),
        P(None, "seq", None),
        P("dp", None, "seq"),
    )
    return jax.shard_map(
        per_device,
        mesh=mesh,
        in_specs=placed,
        out_specs=(P("section", "dp", "seq", None), P("dp", "seq", None), P("seq", None)),
        check_vma=False,
    )
```

```python
import functools

import jax
import jax.numpy as jnp
from jax import lax
from jax.experimental import pallas as pl
from jax.experimental.pallas import tpu as pltpu
from jax.sharding import PartitionSpec as P

HEAD_DIM = 128
GUIDE = 3.0
EPSILON = 1e-06
NEGATIVE = -1e30
SPAN_MOST = 384
LOG2E = 1.4426950408889634
MESH = pl.DeviceIdType.MESH


def attend_kernel(ids_col, ids_row, qkv, out):
    length = qkv.shape[0]
    heads = qkv.shape[1] // (3 * HEAD_DIM)
    rows = min(256, length)
    factor = HEAD_DIM ** (-0.5) * LOG2E
    for block in range(length // rows):
        first = block * rows
        seen = min(length, first + rows + SPAN_MOST)
        hidden = ids_row[:, :seen] > ids_col[first:first + rows, :]
        for head in range(heads):
            base = head * 3 * HEAD_DIM
            query = qkv[first:first + rows, base:base + HEAD_DIM]
            keys = qkv[:seen, base + HEAD_DIM:base + 2 * HEAD_DIM]
            values = qkv[:seen, base + 2 * HEAD_DIM:base + 3 * HEAD_DIM]
            scores = lax.dot_general(
                query, keys, (((1,), (1,)), ((), ())), preferred_element_type=jnp.float32
            )
            scores = jnp.where(hidden, NEGATIVE, scores)
            highest = jnp.max(scores, axis=1, keepdims=True)
            expon = jnp.exp2((scores - highest) * factor)
            total = jnp.sum(expon, axis=1, keepdims=True)
            mixed = jnp.dot(
                expon.astype(jnp.bfloat16), values, preferred_element_type=jnp.float32
            )
            out[first:first + rows, head * HEAD_DIM:(head + 1) * HEAD_DIM] = (
                mixed / total
            ).astype(jnp.bfloat16)


def attend(qkv_rows, frame_ids):
    length, width = qkv_rows.shape
    heads = width // (3 * HEAD_DIM)
    vmem = pl.BlockSpec(memory_space=pltpu.VMEM)
    return pl.pallas_call(
        attend_kernel,
        out_shape=jax.ShapeDtypeStruct((length, heads * HEAD_DIM), jnp.bfloat16),
        in_specs=[vmem] * 3,
        out_specs=vmem,
        compiler_params=pltpu.CompilerParams(vmem_limit_bytes=48 << 20),
        cost_estimate=pl.CostEstimate(
            flops=4 * length * length * HEAD_DIM * heads,
            bytes_accessed=qkv_rows.size * 3,
            transcendentals=length * length * heads,
        ),
    )(frame_ids[:, None], frame_ids[None, :], qkv_rows)


def device_at(section=None, seq=None):
    place = {}
    if section is not None:
        place["section"] = section
    if seq is not None:
        place["seq"] = seq
    return place


def greet(peers):
    barrier = pltpu.get_barrier_semaphore()
    count = 0
    for condition, device in peers:
        if condition is None:
            pl.semaphore_signal(barrier, inc=1, device_id=device, device_id_type=MESH)
            count = count + 1
        else:
            @pl.when(condition)
            def _(device=device):
                pl.semaphore_signal(barrier, inc=1, device_id=device, device_id_type=MESH)

            count = count + condition.astype(jnp.int32)
    pl.semaphore_wait(barrier, count)


def remote(src, dst, send, recv, device):
    return pltpu.make_async_remote_copy(
        src_ref=src, dst_ref=dst, send_sem=send, recv_sem=recv,
        device_id=device, device_id_type=MESH,
    )


def head_kernel(
    sections, line,
    flags, latent, pending, context, w_qkv, w_out, qkv, w_proj,
    inbox, full, outbox, w_all, o_all, w_in,
    z_send, z_recv, plane_send, plane_recv, sib_send, sib_recv, slab_send, slab_recv, load,
):
    section = lax.axis_index("section")
    me = lax.axis_index("seq")
    z, core = lax.div(me, 2), lax.rem(me, 2)
    sibling = device_at(seq=2 * z + 1 - core)
    above = device_at(seq=jnp.minimum(me + 2, 2 * line - 1))
    below = device_at(seq=jnp.maximum(me - 2, 0))
    plane = [device_at(section=lax.rem(section + d, sections)) for d in range(1, sections)]
    has_above, has_below = z < line - 1, z > 0
    greet([(None, sibling), (has_above, above), (has_below, below)] + [(None, p) for p in plane])

    pieces, chunk = inbox.shape[1], inbox.shape[3]
    loads = [
        pltpu.make_async_copy(w_qkv, w_all, load.at[0]),
        pltpu.make_async_copy(w_out, o_all, load.at[1]),
    ]
    for copy in loads:
        copy.start()

    def z_copy(way, block, h):
        return remote(
            inbox.at[block, h], inbox.at[block, h], z_send.at[way, block, h],
            z_recv.at[block, h], above if way == 0 else below,
        )

    for h in range(pieces):
        rows = pl.ds(pl.multiple_of((section * pieces + h) * chunk, chunk), chunk)
        inbox[z, h, 0] = latent[rows, :]
        inbox[z, h, 1] = pending[rows, :]

        @pl.when(has_above)
        def _(h=h):
            z_copy(0, z, h).start()

        @pl.when(has_below)
        def _(h=h):
            z_copy(1, z, h).start()

    def normed(latent_rows, pending_rows, to):
        source = source_of(flags, context, latent_rows, pending_rows, to)
        mean = jnp.mean(source * source, axis=1, keepdims=True)
        return (source * lax.rsqrt(mean + EPSILON)).astype(jnp.bfloat16)

    def own(index, carry):
        q, h = lax.div(index, pieces), lax.rem(index, pieces)
        rows = pl.ds(pl.multiple_of(index * chunk, chunk), chunk)
        full[z, core, q, h] = normed(latent[rows, :], pending[rows, :], section)
        return carry

    lax.fori_loop(0, sections * pieces, own, 0)

    def slab_copy(owner):
        return remote(full.at[z, owner], full.at[z, owner], slab_send, slab_recv, sibling)

    slab_copy(core).start()

    for copy, every, chosen in zip(loads, (w_all, o_all), (w_in, w_proj)):
        copy.wait()
        amount = min(128, chosen.shape[0])

        def choose(index, carry, every=every, chosen=chosen, amount=amount):
            rows = pl.ds(pl.multiple_of(index * amount, amount), amount)
            last = jnp.where(flags[2, 1] > 0.5, every[1, rows, :], every[2, rows, :])
            chosen[rows, :] = jnp.where(flags[2, 0] > 0.5, every[0, rows, :], last)
            return carry

        lax.fori_loop(0, chosen.shape[0] // amount, choose, 0)

    def plane_copy(d, block, h, owner):
        return remote(
            outbox.at[d - 1, block, h], full.at[block, core, owner, h],
            plane_send.at[d - 1, block, h], plane_recv.at[d - 1, block, h], plane[d - 1],
        )

    def sib_copy(block, q, h, owner):
        slot = full.at[block, owner, q, h]
        return remote(slot, slot, sib_send.at[block, q, h], sib_recv.at[block, q, h], sibling)

    def multiply(block):
        rows = full[block].reshape(2 * sections * pieces * chunk, full.shape[-1])
        place = pl.ds(pl.multiple_of(block * rows.shape[0], rows.shape[0]), rows.shape[0])
        for column in range(0, qkv.shape[1], 128):
            qkv[place, column:column + 128] = jnp.dot(
                rows, w_in[:, column:column + 128], preferred_element_type=jnp.float32
            ).astype(jnp.bfloat16)

    def take(block, h, way, onward):
        z_copy(way, block, h).wait_recv()

        @pl.when(onward)
        def _():
            z_copy(way, block, h).start()

        latent_rows, pending_rows = inbox[block, h, 0], inbox[block, h, 1]
        for d in range(1, sections):
            outbox[d - 1, block, h] = normed(
                latent_rows, pending_rows, lax.rem(section + d, sections)
            )
            plane_copy(d, block, h, section).start()
        full[block, core, section, h] = normed(latent_rows, pending_rows, section)
        sib_copy(block, section, h, core).start()

    def pass_on(block, h):
        for d in range(1, sections):
            sender = lax.rem(section + sections - d, sections)
            plane_copy(d, block, h, sender).wait_recv()
            sib_copy(block, sender, h, core).start()

    def finish(block):
        for h in range(pieces):
            for q in range(sections):
                sib_copy(block, q, h, 1 - core).wait_recv()
        multiply(block)

    def step(index, carry):
        k, h = lax.div(index, pieces), lax.rem(index, pieces)

        @pl.when(jnp.logical_and(k < line, z >= k))
        def _():
            take(z - k, h, 0, has_above)

        @pl.when(z + k < line)
        def _():
            take(z + k, h, 1, has_below)

        late = index - 2
        k2, h2 = lax.div(late, pieces), lax.rem(late, pieces)

        @pl.when(jnp.logical_and(k2 >= 1, z >= k2))
        def _():
            pass_on(z - k2, h2)

        @pl.when(jnp.logical_and(k2 >= 1, z + k2 < line))
        def _():
            pass_on(z + k2, h2)

        done = k - 1

        @pl.when(h == 1)
        def _():
            @pl.when(done == 0)
            def _():
                slab_copy(1 - core).wait_recv()
                multiply(z)

            @pl.when(jnp.logical_and(done >= 1, z >= done))
            def _():
                finish(z - done)

            @pl.when(jnp.logical_and(done >= 1, z + done < line))
            def _():
                finish(z + done)

        return carry

    lax.fori_loop(pieces, line * pieces + 2, step, 0)

    slab_copy(core).wait_send()

    def drain(index, carry):
        block, h = lax.div(index, pieces), lax.rem(index, pieces)

        @pl.when(jnp.logical_and(block <= z, has_above))
        def _():
            z_copy(0, block, h).wait_send()

        @pl.when(jnp.logical_and(block >= z, has_below))
        def _():
            z_copy(1, block, h).wait_send()

        @pl.when(block != z)
        def _():
            for d in range(1, sections):
                plane_copy(d, block, h, section).wait_send()
            for q in range(sections):
                sib_copy(block, q, h, core).wait_send()

        return carry

    lax.fori_loop(0, line * pieces, drain, 0)


def head(flags, latent, pending, context, w_qkv, w_out):
    sections, seq = lax.axis_size("section"), lax.axis_size("seq")
    line = seq // 2
    rows, width = latent.shape
    chunk = 16
    pieces = rows // (sections * chunk)
    vmem = pl.BlockSpec(memory_space=pltpu.VMEM)
    smem = pl.BlockSpec(memory_space=pltpu.SMEM)
    dma = pltpu.SemaphoreType.DMA
    bf = jnp.bfloat16
    return pl.pallas_call(
        functools.partial(head_kernel, sections, line),
        out_shape=(
            jax.ShapeDtypeStruct((seq * rows, w_qkv.shape[2]), bf),
            jax.ShapeDtypeStruct(w_out.shape[1:], bf),
        ),
        in_specs=[smem] + [vmem] * 3 + [pl.BlockSpec(memory_space=pl.ANY)] * 2,
        out_specs=(vmem, vmem),
        scratch_shapes=[
            pltpu.VMEM((line, pieces, 2, chunk, width), bf),
            pltpu.VMEM((line, 2, sections, pieces, chunk, width), bf),
            pltpu.VMEM((sections - 1, line, pieces, chunk, width), bf),
            pltpu.VMEM(w_qkv.shape, bf),
            pltpu.VMEM(w_out.shape, bf),
            pltpu.VMEM(w_qkv.shape[1:], bf),
            dma((2, line, pieces)), dma((line, pieces)),
            dma((sections - 1, line, pieces)), dma((sections - 1, line, pieces)),
            dma((line, sections, pieces)), dma((line, sections, pieces)),
            dma(()), dma(()), dma((2,)),
        ],
        compiler_params=pltpu.CompilerParams(
            collective_id=2, has_side_effects=True, vmem_limit_bytes=56 << 20
        ),
        cost_estimate=pl.CostEstimate(
            flops=2 * seq * rows * w_qkv.size // w_qkv.shape[0], bytes_accessed=16 << 20, transcendentals=0
        ),
    )(flags, latent, pending, context, w_qkv, w_out)


def source_of(flags, context, latent_rows, pending_rows, to):
    scored = pending_rows.astype(jnp.float32) + flags[1, to] * context[...]
    generator = flags[0, to]
    return generator * latent_rows.astype(jnp.float32) + (1.0 - generator) * scored


def tail_kernel(
    sections, line, finish,
    scale, flags, attn, w2, latent, pending, context, stored,
    block_out, dmd, grad_out,
    attn_sib, w_sib, arrived, leaving, res_out, branch, terms, parts, grads, lines, finals, stored_t,
    core_send, core_recv, sum_send, sum_recv, plane_send, plane_recv,
    line_send, line_recv, sib_send, sib_recv,
):
    section = lax.axis_index("section")
    me = lax.axis_index("seq")
    z, core = lax.div(me, 2), lax.rem(me, 2)
    sibling = device_at(seq=2 * z + 1 - core)
    above = device_at(seq=jnp.minimum(me + 2, 2 * line - 1))
    below = device_at(seq=jnp.maximum(me - 2, 0))
    plane = [device_at(section=lax.rem(section + d, sections)) for d in range(1, sections)]
    has_above, has_below = z < line - 1, z > 0
    greet([(None, sibling), (has_above, above), (has_below, below)] + [(None, p) for p in plane])

    rows = latent.shape[0]
    both = 2 * rows
    half = w2.shape[1] // 2
    quarter = terms.shape[2]
    per_half = half // quarter
    tiles = quarter // 128
    chunks = min(3, tiles)
    edges = [128 * -(-tiles * j // chunks) for j in range(chunks + 1)]
    widths = [edges[j + 1] - edges[j] for j in range(chunks)]

    def lanes(j):
        return slice(edges[j], edges[j + 1])

    def packed(j, part=None):
        if part is None:
            return slice(per_half * edges[j], per_half * edges[j + 1])
        first = per_half * edges[j] + part * widths[j]
        return slice(first, first + widths[j])

    w_copy = remote(
        w2.at[:, pl.ds(pl.multiple_of((1 - core) * half, 128), half)], w_sib,
        core_send.at[0], core_recv.at[0], sibling)
    a_copy = remote(attn, attn_sib, core_send.at[1], core_recv.at[1], sibling)
    w_copy.start()
    a_copy.start()
    w_copy.wait()
    a_copy.wait()

    def product(first, amount, j, part):
        span = pl.ds(pl.multiple_of(first, rows), amount)
        columns = slice(part * quarter + edges[j], part * quarter + edges[j + 1])
        mine = pl.ds(pl.multiple_of(core * half + columns.start, 128), widths[j])
        return jnp.dot(
            attn[span, :], w2[:, mine], preferred_element_type=jnp.float32
        ) + jnp.dot(
            attn_sib[span, :], w_sib[:, columns], preferred_element_type=jnp.float32
        )

    def sum_copy(j, way, target):
        return remote(
            leaving.at[target, :, packed(j)], arrived.at[way, target, :, packed(j)],
            sum_send.at[j, way, target], sum_recv.at[j, way, target],
            above if way == 0 else below,
        )

    def push(j, way, target, has_before):
        @pl.when(has_before)
        def _():
            sum_copy(j, way, target).wait_recv()

        for part in range(per_half):
            value = product(target * both, both, j, part)
            before = arrived[way, target, :, packed(j, part)].astype(jnp.float32)
            value = value + jnp.where(has_before, before, 0.0)
            leaving[target, :, packed(j, part)] = value.astype(jnp.bfloat16)
        sum_copy(j, way, target).start()

    def pushes(j, first, last):
        def step(tau, carry):
            @pl.when(tau >= z)
            def _():
                push(j, 0, line - 1 - tau + z, has_below)

            @pl.when(tau >= line - 1 - z)
            def _():
                push(j, 1, tau - (line - 1 - z), has_above)

            return carry

        lax.fori_loop(min(first, line - 1), min(last, line - 1), step, 0)

    def res_copy(j, owner):
        return remote(
            res_out.at[:, packed(j)], branch.at[owner, :, packed(j)],
            core_send.at[2 + j], core_recv.at[2 + j], sibling,
        )

    def own_sum(j):
        @pl.when(has_below)
        def _():
            sum_copy(j, 0, z).wait_recv()

        @pl.when(has_above)
        def _():
            sum_copy(j, 1, z).wait_recv()

        def own(which, part):
            span = pl.ds(pl.multiple_of(which * rows, rows), rows)
            value = product(z * both + which * rows, rows, j, part)
            up = arrived[0, z, span, packed(j, part)].astype(jnp.float32)
            down = arrived[1, z, span, packed(j, part)].astype(jnp.float32)
            return value + jnp.where(has_below, up, 0.0) + jnp.where(has_above, down, 0.0)

        for part in range(per_half):
            res_out[:, packed(j, part)] = own(1 - core, part)
        res_copy(j, core).start()
        for part in range(per_half):
            branch[core, :, packed(j, part)] = own(core, part)

    def plane_copies(j, phase, src, dst, which=range(1, sections)):
        return [
            remote(src(lax.rem(section + d, sections)), dst(d),
                   plane_send.at[j, phase, d - 1], plane_recv.at[j, phase, d - 1], plane[d - 1])
            for d in which
        ]

    def term_copies(j):
        return plane_copies(
            j, 0, lambda to: terms.at[to, :, lanes(j)], lambda d: parts.at[d - 1, :, lanes(j)]
        )

    def share(j):
        res_copy(j, core).wait_send()
        res_copy(j, 1 - core).wait_recv()
        for q in range(sections):
            value = branch[q // per_half, :, packed(j, q % per_half)]
            terms[q, :, lanes(j)] = (scale[0, 0] * value).astype(jnp.bfloat16)
        for copy in term_copies(j):
            copy.start()
        for q in range(sections):
            columns = slice(q * quarter + edges[j], q * quarter + edges[j + 1])
            source = source_of(
                flags, context[:, columns], latent[:, columns], pending[:, columns], section
            )
            value = branch[q // per_half, :, packed(j, q % per_half)]
            block_out[:, columns] = (source + value).astype(jnp.bfloat16)

    def line_copy(j, way, block):
        slot = lines.at[block, core, :, lanes(j)]
        return remote(
            slot, slot, line_send.at[j, way, block], line_recv.at[j, way, block],
            above if way == 0 else below,
        )

    def sib_copy(j, block, owner):
        slot = lines.at[block, owner, :, lanes(j)]
        return remote(slot, slot, sib_send.at[j, block], sib_recv.at[j, block], sibling)

    def gather(j, phase, buffer, owner, which=range(1, sections)):
        slot = buffer.at[owner, :, lanes(j)]
        return plane_copies(j, phase, lambda to: slot, lambda d: slot, which)

    def gathered(j, phase, buffer):
        for d in range(1, sections):
            gather(j, phase, buffer, section, [d])[0].wait_send()
            sender = lax.rem(section + sections - d, sections)
            gather(j, phase, buffer, sender, [d])[0].wait_recv()

    def add_up(j):
        total = terms[section, :, lanes(j)].astype(jnp.float32)
        copies = term_copies(j)
        for d in range(1, sections):
            copies[d - 1].wait()
            total = total + parts[d - 1, :, lanes(j)].astype(jnp.float32)
        grad = total.astype(jnp.bfloat16)
        lines[z, core, :, lanes(j)] = grad
        grads[section, :, lanes(j)] = grad

        @pl.when(has_above)
        def _():
            line_copy(j, 0, z).start()

        @pl.when(has_below)
        def _():
            line_copy(j, 1, z).start()

        sib_copy(j, z, core).start()
        for copy in gather(j, 1, grads, section):
            copy.start()

    def spread(j):
        def step(k, carry):
            @pl.when(z >= k)
            def _():
                line_copy(j, 0, z - k).wait_recv()

                @pl.when(has_above)
                def _():
                    line_copy(j, 0, z - k).start()

                sib_copy(j, z - k, core).start()

            @pl.when(z + k < line)
            def _():
                line_copy(j, 1, z + k).wait_recv()

                @pl.when(has_below)
                def _():
                    line_copy(j, 1, z + k).start()

                sib_copy(j, z + k, core).start()

            return carry

        lax.fori_loop(1, line, step, 0)

    def project(j):
        def sib_wait(block, carry):
            sib_copy(j, block, core).wait_send()
            sib_copy(j, block, 1 - core).wait_recv()
            return carry

        lax.fori_loop(0, line, sib_wait, 0)
        everything = lines[:, :, :, lanes(j)].reshape(line * both, widths[j])
        local = jnp.dot(stored_t[...], everything, preferred_element_type=jnp.float32)
        if finish:
            finals[section, :, lanes(j)] = local.astype(jnp.bfloat16)
            for copy in gather(j, 2, finals, section):
                copy.start()
        else:
            grad_out[:, lanes(j)] = local

    pushes(0, 0, line)
    stored_t[...] = stored[...].T
    for j in range(chunks):
        if j + 1 < chunks:
            pushes(j + 1, 0, 1)
        own_sum(j)
        if j + 1 < chunks:
            pushes(j + 1, 1, 2)
        share(j)
        if j >= 1:
            spread(j - 1)
        if j + 1 < chunks:
            pushes(j + 1, 2, line)
        add_up(j)
        if j >= 1:
            project(j - 1)
    spread(chunks - 1)
    project(chunks - 1)

    for j in range(chunks):
        gathered(j, 1, grads)
        for q in range(sections):
            columns = slice(q * quarter + edges[j], q * quarter + edges[j + 1])
            dmd[:, columns] = grads[q, :, lanes(j)]

    def line_drain(block, carry):
        for j in range(chunks):
            @pl.when(jnp.logical_and(block <= z, has_above))
            def _(j=j):
                line_copy(j, 0, block).wait_send()

            @pl.when(jnp.logical_and(block >= z, has_below))
            def _(j=j):
                line_copy(j, 1, block).wait_send()

            @pl.when(block > z)
            def _(j=j):
                sum_copy(j, 0, block).wait_send()

            @pl.when(block < z)
            def _(j=j):
                sum_copy(j, 1, block).wait_send()

        return carry

    lax.fori_loop(0, line, line_drain, 0)
    if finish:
        for j in range(chunks):
            gathered(j, 2, finals)
            for q in range(sections):
                columns = slice(q * quarter + edges[j], q * quarter + edges[j + 1])
                grad_out[:, columns] = finals[q, :, lanes(j)]


def tail(scale, flags, attn, w_proj, latent, pending, context, stored, finish):
    sections, seq = lax.axis_size("section"), lax.axis_size("seq")
    line = seq // 2
    rows, width = latent.shape
    length, inner = attn.shape
    half, quarter = width // 2, width // sections
    vmem = pl.BlockSpec(memory_space=pltpu.VMEM)
    smem = pl.BlockSpec(memory_space=pltpu.SMEM)
    bf, f32 = jnp.bfloat16, jnp.float32
    dma = pltpu.SemaphoreType.DMA
    return pl.pallas_call(
        functools.partial(tail_kernel, sections, line, finish),
        out_shape=(
            jax.ShapeDtypeStruct((rows, width), bf),
            jax.ShapeDtypeStruct((rows, width), bf),
            jax.ShapeDtypeStruct((inner, width if finish else quarter), bf if finish else f32),
        ),
        in_specs=[smem] * 2 + [vmem] * 6,
        out_specs=(vmem,) * 3,
        scratch_shapes=[
            pltpu.VMEM((length, inner), bf),
            pltpu.VMEM((inner, half), bf),
            pltpu.VMEM((2, line, 2 * rows, half), bf),
            pltpu.VMEM((line, 2 * rows, half), bf),
            pltpu.VMEM((rows, half), f32),
            pltpu.VMEM((2, rows, half), f32),
            pltpu.VMEM((sections, rows, quarter), bf),
            pltpu.VMEM((sections - 1, rows, quarter), bf),
            pltpu.VMEM((sections, rows, quarter), bf),
            pltpu.VMEM((line, 2, rows, quarter), bf),
            pltpu.VMEM((sections, inner, quarter), bf),
            pltpu.VMEM((inner, length), bf),
            dma((5,)), dma((5,)),
            dma((3, 2, line)), dma((3, 2, line)),
            dma((3, 3, sections - 1)), dma((3, 3, sections - 1)),
            dma((3, 2, line)), dma((3, 2, line)),
            dma((3, line)), dma((3, line)),
        ],
        compiler_params=pltpu.CompilerParams(
            collective_id=1, has_side_effects=True, vmem_limit_bytes=56 << 20
        ),
        cost_estimate=pl.CostEstimate(
            flops=2 * length * inner * width, bytes_accessed=8 << 20, transcendentals=0
        ),
    )(scale, flags, attn, w_proj, latent, pending, context, stored)


def per_device(roles, block_ids, latent, pending, context, w_qkv, w_out, stored_attn):
    section = lax.axis_index("section")
    places = jnp.arange(4, dtype=jnp.int32)
    weight_table = jnp.array([0.0, -GUIDE, GUIDE - 1.0, 1.0], jnp.float32)
    section_role = jnp.sum(jnp.where(places == section, roles, 0))
    model_index = jnp.sum(jnp.where(places == section_role, jnp.array([0, 1, 1, 2], jnp.int32), 0))
    score_weight = jnp.sum(jnp.where(places == section_role, weight_table, 0.0))
    is_generator = section_role == 0
    flags = jnp.stack(
        [roles == 0, jnp.logical_or(roles == 1, roles == 3), places == model_index]
    ).astype(jnp.float32)
    qkv_rows, w_proj = head(flags, latent[0], pending[0], context, w_qkv, w_out)
    frame_ids = jnp.where(is_generator, block_ids[0, 0], block_ids[1, 0])
    attn = attend(qkv_rows, frame_ids)
    finish = lax.axis_size("dp") == 1
    block_out, gradient, grad_out = tail(
        score_weight.reshape(1, 1), flags, attn, w_proj, latent[0], pending[0], context,
        stored_attn[0], finish,
    )
    if not finish:
        grad_out = lax.psum(grad_out, "dp").astype(jnp.bfloat16)
        grad_out = lax.all_gather(grad_out, "section", axis=1, tiled=True)
    return (
        block_out[None, None], gradient[None].astype(jnp.float32), grad_out.astype(jnp.float32)
    )


def solution(mesh):
    placed = (
        P(),
        P(None, "dp", None),
        P("dp", "seq", None),
        P("dp", "seq", None),
        P("dp", None),
        P(None, None, "seq"),
        P(None, "seq", None),
        P("dp", None, "seq"),
    )
    return jax.shard_map(
        per_device,
        mesh=mesh,
        in_specs=placed,
        out_specs=(P("section", "dp", "seq", None), P("dp", "seq", None), P("seq", None)),
        check_vma=False,
    )
```
